32 devices in a mesh: depth: 8 (over z, x), height: 4 (over y, core).
Axes of the slice: x: 2, y: 2, z: 4, core: 2. Of those that a mesh axis runs over, the one named last changes fastest.
Arguments:
- queries: bfloat16 [1792, 512], P('depth', 'height'), may hold values from -6 to 6
- key_vectors: bfloat16 [1792, 512], P('depth', 'height'), may hold values from -6 to 6
- value_vectors: bfloat16 [1792, 512], P('depth', 'height'), may hold values from -6 to 6
- grad_conv: bfloat16 [16, 16, 56, 256], P('depth', 'height'), may hold values from -6 to 6
- conv_weight: bfloat16 [3, 3, 3, 256, 256], replicated, may hold values from -0.078125 to 0.078125
- dec_weight: bfloat16 [512, 8, 256], replicated, may hold values from -0.125 to 0.125
Outputs:
- grad_queries: bfloat16 [1792, 512], P('depth', 'height')
- grad_keys: bfloat16 [1792, 512], P('depth', 'height')
- grad_values: bfloat16 [1792, 512], P('depth', 'height')
The draws below stay inside these ranges and needn't reach their ends.
All inputs are finite; a program needn't handle non-finite values.
Results may differ from the reference program's by a relative error of at most 0.024.
Values may be sent and summed in bfloat16 or wider, within the bound.
A program may use at most 128 MiB of HBM per device.

```python
import math
import jax
import jax.numpy as jnp
from jax import lax

C = 256
HEADS = 8
HSZ = 64
HT = 8
WT = 28
HD = 512
TOKENS = 1792
N_DEPTH = 8


def draw_queries(key, part):
    own_key = jax.random.fold_in(key, 11)
    drawn = jnp.clip(jax.random.normal(own_key, (TOKENS, HEADS * HSZ), jnp.float32), -6.0, 6.0)
    return drawn.astype(jnp.bfloat16)


def draw_key_vectors(key, part):
    own_key = jax.random.fold_in(key, 23)
    drawn = jnp.clip(jax.random.normal(own_key, (TOKENS, HEADS * HSZ), jnp.float32), -6.0, 6.0)
    return drawn.astype(jnp.bfloat16)


def draw_value_vectors(key, part):
    own_key = jax.random.fold_in(key, 31)
    column_key = jax.random.fold_in(key, 37)
    column_mean = jax.random.normal(column_key, (1, HEADS * HSZ), jnp.float32)
    noise = jax.random.normal(own_key, (TOKENS, HEADS * HSZ), jnp.float32)
    return jnp.clip(column_mean + noise, -6.0, 6.0).astype(jnp.bfloat16)


def levels(stream_key, extent, shards, least, high):
    gain = 1.0
    for position, shards_of in shards:
        heights = jax.random.uniform(jax.random.fold_in(jax.random.fold_in(stream_key, 6), position), (shards_of,), jnp.float32, least / len(shards), high / len(shards))
        gain = gain * jnp.repeat(jnp.exp(heights), extent[position] // shards_of).reshape((-1,) + (1,) * (len(extent) - 1 - position))
    return gain


def centred(key, extent, spread, most, cuts=(), held_as=jnp.bfloat16):
    factor_of = levels(key, extent, cuts, -0.22, 0.18) if cuts else 1.0
    array = jax.random.normal(key, extent, jnp.float32) * spread * factor_of
    return jnp.minimum(jnp.maximum(array, -most), most).astype(held_as)


def setup_inputs(seed: int = 0) -> dict:
    key_of = jax.random.split(jax.random.key(seed), 7)
    return {
        "queries": draw_queries(jax.random.fold_in(key_of[6], 71), 0),
        "key_vectors": draw_key_vectors(jax.random.fold_in(key_of[6], 71), 0),
        "value_vectors": draw_value_vectors(jax.random.fold_in(key_of[6], 71), 0),
        "grad_conv": centred(key_of[3], (2 * TOKENS // (HT * WT), 2 * HT, 2 * WT, C), 1.0, 6.0, ((0, 8), (1, 4))),
        "conv_weight": centred(key_of[4], (3, 3, 3, C, C), (27 * C) ** -0.5, 0.078125),
        "dec_weight": centred(key_of[5], (HD, 8, C), (8 * C) ** -0.5, 0.125),
    }


LOSS_SCALE = 64.0

def conv_grads(grad_conv, conv_weight):
    volume = grad_conv.astype(jnp.float32)
    padded = jnp.pad(volume, ((1, 1), (1, 1), (1, 1), (0, 0)))
    depth_len = volume.shape[0]
    rows_len = volume.shape[1]
    cols_len = volume.shape[2]
    kernel = conv_weight.astype(jnp.float32)
    summed = jnp.zeros(volume.shape, jnp.float32)
    for along_depth in range(3):
        for along_rows in range(3):
            for along_cols in range(3):
                window = padded[2 - along_depth:2 - along_depth + depth_len, 2 - along_rows:2 - along_rows + rows_len, 2 - along_cols:2 - along_cols + cols_len]
                summed = summed + jnp.einsum('dhwc,ec->dhwe', window, kernel[along_depth, along_rows, along_cols], precision=lax.Precision.HIGHEST)
    return (LOSS_SCALE * summed).astype(jnp.bfloat16)

def output_grads(voxel_grads, dec_weight):
    grouped = voxel_grads.reshape(N_DEPTH, 2, HT, 2, WT, 2, C)
    grouped = grouped.transpose(0, 2, 4, 1, 3, 5, 6).reshape(TOKENS, 8 * C)
    decoder = dec_weight.reshape(HEADS * HSZ, 8 * C)
    return jnp.dot(grouped, decoder.T, preferred_element_type=jnp.float32).astype(jnp.bfloat16)

def attention_grads(queries, key_vectors, value_vectors, out_grads):
    head_scale = 1.0 / math.sqrt(HSZ)
    query_all = queries.astype(jnp.float32).reshape(TOKENS, HEADS, HSZ)
    key_all = key_vectors.astype(jnp.float32).reshape(TOKENS, HEADS, HSZ)
    value_all = value_vectors.astype(jnp.float32).reshape(TOKENS, HEADS, HSZ)
    grad_all = out_grads.astype(jnp.float32).reshape(TOKENS, HEADS, HSZ)
    block_len = HT * WT

    def sweep(carried, block_index):
        key_acc, value_acc = carried
        row_start = (block_index * block_len).astype(jnp.int32)
        query_rows = lax.dynamic_slice_in_dim(query_all, row_start, block_len, 0)
        grad_block = lax.dynamic_slice_in_dim(grad_all, row_start, block_len, 0)
        logits = jnp.einsum('qhd,khd->hqk', query_rows, key_all) * head_scale
        row_max = lax.optimization_barrier(jnp.max(logits, axis=2, keepdims=True))
        log_norm = row_max + jnp.log(lax.optimization_barrier(jnp.sum(jnp.exp(logits - row_max), axis=2, keepdims=True)))
        softmax_rows = jnp.exp(logits - log_norm)
        slopes = jnp.einsum('qhd,khd->hqk', grad_block, value_all)
        delta_rows = lax.optimization_barrier(jnp.sum(softmax_rows * slopes, axis=2, keepdims=True))
        score_grads = lax.optimization_barrier((softmax_rows * (slopes - delta_rows)).astype(jnp.bfloat16)).astype(jnp.float32)
        prob_rows = lax.optimization_barrier(softmax_rows.astype(jnp.bfloat16)).astype(jnp.float32)
        query_part = jnp.einsum('hqk,khd->qhd', score_grads, key_all) * head_scale
        key_acc = key_acc + jnp.einsum('hqk,qhd->khd', score_grads, query_rows) * head_scale
        value_acc = value_acc + jnp.einsum('hqk,qhd->khd', prob_rows, grad_block)
        return ((key_acc, value_acc), query_part)
    start_acc = jnp.zeros((TOKENS, HEADS, HSZ), jnp.float32)
    final_accs, query_parts = lax.scan(sweep, (start_acc, start_acc), jnp.arange(N_DEPTH, dtype=jnp.int32))
    grad_queries = query_parts.reshape(TOKENS, HEADS * HSZ).astype(jnp.bfloat16)
    grad_keys = final_accs[0].reshape(TOKENS, HEADS * HSZ).astype(jnp.bfloat16)
    grad_values = final_accs[1].reshape(TOKENS, HEADS * HSZ).astype(jnp.bfloat16)
    return (grad_queries, grad_keys, grad_values)

def reference(queries, key_vectors, value_vectors, grad_conv, conv_weight, dec_weight):
    voxel_grads = conv_grads(grad_conv, conv_weight)
    out_grads = output_grads(voxel_grads, dec_weight)
    grad_queries, grad_keys, grad_values = attention_grads(queries, key_vectors, value_vectors, out_grads)
    return (grad_queries, grad_keys, grad_values)
```

```python
import functools
import math

import jax
import jax.numpy as jnp
from jax import lax
from jax.experimental import pallas as pl
from jax.experimental.pallas import tpu as pltpu
from jax.sharding import PartitionSpec as P

HSZ = 64
LOSS_SCALE = 64.0
MESH = pl.DeviceIdType.MESH
BF = jnp.bfloat16
F32 = jnp.float32
KEYS, VALUES, QUERIES, GRADS = range(4)


def round_up(value, multiple):
    return (value + multiple - 1) // multiple * multiple


def dot_nt(left, right):
    return lax.dot_general(left, right, (((1,), (1,)), ((), ())), preferred_element_type=F32)


def dot_nn(left, right):
    return lax.dot_general(left, right, (((1,), (0,)), ((), ())), preferred_element_type=F32)


def selection(shape, runs):
    row = lax.broadcasted_iota(jnp.int32, shape, 0)
    col = lax.broadcasted_iota(jnp.int32, shape, 1)
    chosen = None
    for first, count, start, step in runs:
        hit = (row >= first) & (row < first + count) & (col == start + step * (row - first))
        chosen = hit if chosen is None else chosen | hit
    return chosen.astype(F32).astype(BF)


def kernel(
    depth, height, inner,
    q_ref, k_ref, v_ref, x_ref, w_hbm, d_hbm,
    dq_ref, dk_ref, dv_ref,
    halo, w_ref, d_ref, voxels, pieces, landed, blocks, stats, probs, dq_acc, dk_acc, dv_acc,
    load_sems, halo_send, halo_recv, swap_send, swap_recv,
    own_send, pair_send, forward_send, block_recv, stat_send, stat_recv,
):
    planes, rows, cols, channels = x_ref.shape
    colp = halo.shape[2]
    tokens, width = q_ref.shape
    heads = width // HSZ
    scale = 1.0 / math.sqrt(HSZ)
    outer = depth // inner
    tok_rows, tok_cols = rows // 2, cols // 2
    toks = tok_rows * tok_cols
    tokp = pieces.shape[1]

    d = lax.axis_index("depth")
    h = lax.axis_index("height")
    z, x = d // inner, d % inner
    other = inner * z + (inner - 1 - x)

    def line(step):
        return ((z + step) % outer) * inner + x

    def across(step):
        return ((z + step) % outer) * inner + (inner - 1 - x)

    load_w = pltpu.make_async_copy(w_hbm, w_ref, load_sems.at[0])
    load_d = pltpu.make_async_copy(d_hbm, d_ref, load_sems.at[1])
    load_w.start()
    load_d.start()

    halo[...] = jnp.zeros_like(halo)
    halo[1 : 1 + planes, 1 : 1 + rows, 0:cols, :] = x_ref[...]

    barrier = pltpu.get_barrier_semaphore()

    def greet(dd, hh):
        pl.semaphore_signal(barrier, inc=1, device_id=(dd, hh), device_id_type=MESH)

    for step in range(1, height):
        greet(d, (h + step) % height)

    def greet_line(step, carry):
        greet(line(step), h)
        return carry

    lax.fori_loop(1, outer, greet_line, 0)
    if inner == 2:
        def greet_across(step, carry):
            greet(across(step), h)
            return carry
        lax.fori_loop(0, outer, greet_across, 0)

    corners = [(dz, dy) for dz in (-1, 1) for dy in (-1, 1)]
    sides = [(dz, 0) for dz in (-1, 1)] + [(0, dy) for dy in (-1, 1)]

    def exists(dz, dy):
        found = None
        for delta, place, extent in ((dz, d, depth), (dy, h, height)):
            if delta:
                here = (place + delta >= 0) & (place + delta < extent)
                found = here if found is None else found & here
        return found

    count = (height - 1) + (outer - 1) + (outer if inner == 2 else 0)
    for dz, dy in corners:
        there = exists(dz, dy)
        count = count + jnp.where(there, 1, 0)

        @pl.when(there)
        def _(dz=dz, dy=dy):
            greet(d + dz, h + dy)

    pl.semaphore_wait(barrier, count)

    def span(delta, extent, receiving):
        if delta == 0:
            return pl.ds(1, extent)
        if receiving:
            return pl.ds(0 if delta > 0 else extent + 1, 1)
        return pl.ds(extent if delta > 0 else 1, 1)

    def halo_copy(index, dz, dy):
        return pltpu.make_async_remote_copy(
            src_ref=halo.at[span(dz, planes, False), span(dy, rows, False)],
            dst_ref=halo.at[span(dz, planes, True), span(dy, rows, True)],
            send_sem=halo_send.at[index],
            recv_sem=halo_recv.at[index],
            device_id=(d + dz, h + dy),
            device_id_type=MESH,
        )

    ways = sides + corners
    for index, (dz, dy) in enumerate(ways):
        @pl.when(exists(dz, dy))
        def _(index=index, dz=dz, dy=dy):
            halo_copy(index, dz, dy).start()

    sources = {KEYS: k_ref, VALUES: v_ref, QUERIES: q_ref}

    def block_copy(array, slot, send_sem, target):
        return pltpu.make_async_remote_copy(
            src_ref=blocks.at[array, slot],
            dst_ref=blocks.at[array, slot],
            send_sem=send_sem,
            recv_sem=block_recv.at[array, slot],
            device_id=(target, h),
            device_id_type=MESH,
        )

    def send_own(array):
        def one(step, carry):
            block_copy(array, d, own_send.at[array, step], line(step)).start()
            return carry
        lax.fori_loop(1, outer, one, 0)
        if inner == 2:
            block_copy(array, d, pair_send.at[array], other).start()

    def forward(array):
        def one(step, carry):
            slot = line(step)
            block_copy(array, slot, forward_send.at[array, step], other).wait_recv()
            if inner == 2:
                block_copy(array, slot, forward_send.at[array, step], other).start()
            return carry
        lax.fori_loop(1, outer, one, 0)

    def wait_across(array):
        def one(step, carry):
            slot = across(step)
            block_copy(array, slot, pair_send.at[array], other).wait_recv()
            return carry
        if inner == 2:
            lax.fori_loop(0, outer, one, 0)

    for array in (KEYS, VALUES, QUERIES):
        blocks[array, d] = sources[array][...]
        send_own(array)

    for index, (dz, dy) in enumerate(ways):
        @pl.when(exists(-dz, -dy))
        def _(index=index, dz=dz, dy=dy):
            halo_copy(index, dz, dy).wait_recv()
    load_w.wait()
    flat = planes * rows * colp
    total = None
    for l in range(3):
        part = None
        for i in range(3):
            for j in range(3):
                window = halo[2 - i : 2 - i + planes, 2 - j : 2 - j + rows].reshape(flat, channels)
                term = dot_nt(window, w_ref[i, j, l])
                part = term if part is None else part + term
        if l != 1:
            part = pltpu.roll(part, (flat - 1) if l == 0 else 1, 0)
        total = part if total is None else total + part
    voxels[...] = (LOSS_SCALE * total).astype(BF).reshape(planes, rows, colp, channels)

    load_d.wait()
    total = None
    for c in range(2):
        part = None
        for a in range(2):
            for b in range(2):
                lhs = jnp.concatenate([voxels[a, 2 * t + b] for t in range(tok_rows)], axis=0)
                term = dot_nt(lhs, d_ref[4 * a + 2 * b + c])
                part = term if part is None else part + term
        if c == 1:
            part = pltpu.roll(part, tok_rows * colp - 1, 0)
        total = part if total is None else total + part
    pick = selection(
        (tokp, tok_rows * colp), [(t * tok_cols, tok_cols, t * colp, 2) for t in range(tok_rows)]
    )
    compact = dot_nn(pick, total.astype(BF)).astype(BF)
    for hh in range(height):
        pieces[hh] = compact[:, hh * width : (hh + 1) * width]

    def swap_copy(step):
        target = (h + step) % height
        return pltpu.make_async_remote_copy(
            src_ref=pieces.at[target],
            dst_ref=landed.at[h],
            send_sem=swap_send.at[step],
            recv_sem=swap_recv.at[step],
            device_id=(d, target),
            device_id_type=MESH,
        )

    for step in range(1, height):
        swap_copy(step).start()
    landed[h] = pieces[h]
    forward(KEYS)
    forward(VALUES)
    for step in range(1, height):
        swap_copy(step).wait_recv()
    spread = selection((tokens, height * tokp), [(s * toks, toks, s * tokp, 1) for s in range(height)])
    g_own = dot_nn(spread, landed[...].reshape(height * tokp, width)).astype(BF)
    blocks[GRADS, d] = g_own
    send_own(GRADS)
    forward(QUERIES)

    wait_across(KEYS)
    wait_across(VALUES)
    lane = lax.broadcasted_iota(jnp.int32, (tokens, width), 1)
    masks = [(lane >= n * HSZ) & (lane < (n + 1) * HSZ) for n in range(heads)]

    def masked(block, factor=1.0):
        wide = block.astype(F32) * factor
        return [jnp.where(mask, wide, 0.0).astype(BF) for mask in masks]

    def merged(parts):
        result = parts[0]
        for n in range(1, heads):
            result = jnp.where(masks[n], parts[n], result)
        return result

    q_heads = masked(q_ref[...], scale)
    g_heads = masked(g_own)

    def max_step(slot, carry):
        keys = blocks[KEYS, slot]
        return tuple(jnp.maximum(carry[n], dot_nt(q_heads[n], keys)) for n in range(heads))

    low = jnp.full((tokens, tokens), -1e30, F32)
    tops = lax.fori_loop(0, depth, max_step, (low,) * heads)
    tops = [jnp.max(top, axis=1, keepdims=True) for top in tops]

    for n in range(heads):
        dq_acc[n] = jnp.zeros((tokens, width), F32)
        dk_acc[n] = jnp.zeros((tokens, width), F32)
        dv_acc[n] = jnp.zeros((tokens, width), F32)

    def sum_step(slot, carry):
        keys = blocks[KEYS, slot]
        values = blocks[VALUES, slot]
        sums = []
        for n in range(heads):
            weights = jnp.exp(dot_nt(q_heads[n], keys) - tops[n])
            rounded = weights.astype(BF)
            probs[slot, n] = rounded
            dq_acc[n] += dot_nn(rounded, values)
            sums.append(carry[n] + weights)
        return tuple(sums)

    sums = lax.fori_loop(0, depth, sum_step, (jnp.zeros((tokens, tokens), F32),) * heads)
    sums = [jnp.sum(total, axis=1, keepdims=True) for total in sums]
    inverse = [1.0 / total for total in sums]
    out = merged([dq_acc[n] * inverse[n] for n in range(heads)])
    product = g_own.astype(F32) * out
    deltas = [jnp.sum(jnp.where(mask, product, 0.0), axis=1, keepdims=True) for mask in masks]
    columns = [tops[n] + jnp.log(sums[n]) for n in range(heads)] + deltas
    table = jnp.zeros((tokens, width), F32)
    for n, column in enumerate(columns):
        table = jnp.where(lane == n, column, table)
    padded = stats.shape[2]
    if padded > tokens:
        table = jnp.concatenate([table, jnp.zeros((padded - tokens, width), F32)], axis=0)
    stats[d] = table.T[: stats.shape[1]]

    def stat_copy(step):
        return pltpu.make_async_remote_copy(
            src_ref=stats.at[d],
            dst_ref=stats.at[d],
            send_sem=stat_send.at[step],
            recv_sem=stat_recv.at[d],
            device_id=((d + step) % depth, h),
            device_id_type=MESH,
        )

    def stat_wait(slot):
        pltpu.make_async_remote_copy(
            src_ref=stats.at[slot],
            dst_ref=stats.at[slot],
            send_sem=stat_send.at[0],
            recv_sem=stat_recv.at[slot],
            device_id=(slot, h),
            device_id_type=MESH,
        ).wait_recv()

    def stat_start(step, carry):
        stat_copy(step).start()
        return carry

    lax.fori_loop(1, depth, stat_start, 0)
    forward(GRADS)

    for n in range(heads):
        dq_acc[n] = jnp.zeros((tokens, width), F32)

    def query_step(slot, carry):
        keys = blocks[KEYS, slot]
        values = blocks[VALUES, slot]
        for n in range(heads):
            slopes = dot_nt(g_heads[n], values)
            score = (probs[slot, n].astype(F32) * (slopes - deltas[n])).astype(BF)
            dq_acc[n] += dot_nn(score, keys)
        return carry

    lax.fori_loop(0, depth, query_step, 0)
    dq_ref[...] = (merged([dq_acc[n] * inverse[n] for n in range(heads)]) * scale).astype(BF)

    k_heads = masked(k_ref[...], scale)
    v_heads = masked(v_ref[...])

    def owner_block(slot):
        queries = blocks[QUERIES, slot]
        grads = blocks[GRADS, slot]
        table = stats[slot]
        for n in range(heads):
            norm = table[n : n + 1, :tokens]
            delta = table[heads + n : heads + n + 1, :tokens]
            weights = jnp.exp(dot_nt(k_heads[n], queries) - norm)
            score = (weights * (dot_nt(v_heads[n], grads) - delta)).astype(BF)
            dk_acc[n] += dot_nn(score, queries)
            dv_acc[n] += dot_nn(weights.astype(BF), grads)

    def line_step(step, carry):
        slot = line(step)

        @pl.when(step > 0)
        def _():
            stat_wait(slot)

        owner_block(slot)
        return carry

    lax.fori_loop(0, outer, line_step, 0)

    def across_step(step, carry):
        slot = across(step)
        block_copy(QUERIES, slot, pair_send.at[QUERIES], other).wait_recv()
        block_copy(GRADS, slot, pair_send.at[GRADS], other).wait_recv()
        stat_wait(slot)
        owner_block(slot)
        return carry

    if inner == 2:
        lax.fori_loop(0, outer, across_step, 0)
    dk_ref[...] = (merged([dk_acc[n] for n in range(heads)]) * scale).astype(BF)
    dv_ref[...] = merged([dv_acc[n] for n in range(heads)]).astype(BF)

    for index, (dz, dy) in enumerate(ways):
        @pl.when(exists(dz, dy))
        def _(index=index, dz=dz, dy=dy):
            halo_copy(index, dz, dy).wait_send()
    for step in range(1, height):
        swap_copy(step).wait_send()

    def drain_line(step, carry):
        for array in range(4):
            block_copy(array, d, own_send.at[array, step], line(step)).wait_send()
            if inner == 2:
                block_copy(array, line(step), forward_send.at[array, step], other).wait_send()
        return carry

    lax.fori_loop(1, outer, drain_line, 0)
    if inner == 2:
        for array in range(4):
            block_copy(array, d, pair_send.at[array], other).wait_send()

    def drain_stats(step, carry):
        stat_copy(step).wait_send()
        return carry

    lax.fori_loop(1, depth, drain_stats, 0)


def body(mesh_sizes, queries, key_vectors, value_vectors, grad_conv, conv_weight, dec_weight):
    depth, height = mesh_sizes
    inner = 2 if depth % 2 == 0 else 1
    outer = depth // inner
    planes, rows, cols, channels = grad_conv.shape
    colp = round_up(cols + 1, 16)
    tokens, width = queries.shape
    heads = width // HSZ
    tokp = round_up((rows // 2) * (cols // 2), 16)
    features = dec_weight.shape[0]
    decoder = dec_weight.transpose(1, 0, 2)
    out = jax.ShapeDtypeStruct((tokens, width), BF)
    vmem = pl.BlockSpec(memory_space=pltpu.VMEM)
    hbm = pl.BlockSpec(memory_space=pl.ANY)
    dma = pltpu.SemaphoreType.DMA
    return pl.pallas_call(
        functools.partial(kernel, depth, height, inner),
        out_shape=(out, out, out),
        in_specs=[vmem, vmem, vmem, vmem, hbm, hbm],
        out_specs=(vmem, vmem, vmem),
        scratch_shapes=[
            pltpu.VMEM((planes + 2, rows + 2, colp, channels), BF),
            pltpu.VMEM(conv_weight.shape, BF),
            pltpu.VMEM((8, features, channels), BF),
            pltpu.VMEM((planes, rows, colp, channels), BF),
            pltpu.VMEM((height, tokp, width), BF),
            pltpu.VMEM((height, tokp, width), BF),
            pltpu.VMEM((4, depth, tokens, width), BF),
            pltpu.VMEM((depth, round_up(2 * heads, 8), round_up(tokens, 128)), F32),
            pltpu.VMEM((depth, heads, tokens, tokens), BF),
            pltpu.VMEM((heads, tokens, width), F32),
            pltpu.VMEM((heads, tokens, width), F32),
            pltpu.VMEM((heads, tokens, width), F32),
            dma((2,)),
            dma((8,)),
            dma((8,)),
            dma((height,)),
            dma((height,)),
            dma((4, outer)),
            dma((4,)),
            dma((4, outer)),
            dma((4, depth)),
            dma((depth,)),
            dma((depth,)),
        ],
        compiler_params=pltpu.CompilerParams(
            collective_id=0, has_side_effects=True, vmem_limit_bytes=58 * 2**20
        ),
        cost_estimate=pl.CostEstimate(
            flops=4 * 10**9, bytes_accessed=8 * 10**6, transcendentals=2 * 10**6
        ),
    )(queries, key_vectors, value_vectors, grad_conv, conv_weight, decoder)


def solution(mesh):
    in_specs = (
        P("depth", "height"),
        P("depth", "height"),
        P("depth", "height"),
        P("depth", "height", None, None),
        P(),
        P(),
    )
    out_specs = (P("depth", "height"), P("depth", "height"), P("depth", "height"))
    sizes = (mesh.shape["depth"], mesh.shape["height"])
    return jax.shard_map(
        functools.partial(body, sizes),
        mesh=mesh,
        in_specs=in_specs,
        out_specs=out_specs,
        check_vma=False,
    )
```

```python
import functools
import math

import jax
import jax.numpy as jnp
from jax import lax
from jax.experimental import pallas as pl
from jax.experimental.pallas import tpu as pltpu
from jax.sharding import PartitionSpec as P

HSZ = 64
LOSS_SCALE = 64.0
MESH = pl.DeviceIdType.MESH
BF = jnp.bfloat16
F32 = jnp.float32
KEYS, VALUES, QUERIES, GRADS = range(4)


def round_up(value, multiple):
    return (value + multiple - 1) // multiple * multiple


def dot_nt(left, right):
    return lax.dot_general(left, right, (((1,), (1,)), ((), ())), preferred_element_type=F32)


def dot_nn(left, right):
    return lax.dot_general(left, right, (((1,), (0,)), ((), ())), preferred_element_type=F32)


def selection(shape, runs):
    row = lax.broadcasted_iota(jnp.int32, shape, 0)
    col = lax.broadcasted_iota(jnp.int32, shape, 1)
    chosen = None
    for first, count, start, step in runs:
        hit = (row >= first) & (row < first + count) & (col == start + step * (row - first))
        chosen = hit if chosen is None else chosen | hit
    return chosen.astype(F32).astype(BF)


def kernel(
    depth, height,
    q_ref, k_ref, v_ref, x_ref, w_hbm, d_hbm,
    dq_ref, dk_ref, dv_ref,
    halo, w_ref, d_raw, d_tall, d_ref, voxels, pieces, landed, swapped, blocks, stats, probs,
    acc, results, returned,
    load_sems, halo_send, halo_recv, piece_send, piece_recv, swap_send, swap_recv,
    own_send, block_recv, stat_send, stat_recv, return_send, return_recv,
):
    planes, rows, cols, channels = x_ref.shape
    colp = halo.shape[2]
    tokens, width = q_ref.shape
    scale = 1.0 / math.sqrt(HSZ)
    outer = depth // 2
    tok_rows, tok_cols = rows // 2, cols // 2
    toks = tok_rows * tok_cols
    tokp = pieces.shape[1]

    d = lax.axis_index("depth")
    h = lax.axis_index("height")
    z, x = d // 2, d % 2
    other = 2 * z + (1 - x)

    load_w = pltpu.make_async_copy(w_hbm, w_ref, load_sems.at[0])
    load_d = pltpu.make_async_copy(d_hbm, d_raw, load_sems.at[1])
    load_w.start()
    load_d.start()

    halo[...] = jnp.zeros_like(halo)
    halo[1 : 1 + planes, 1 : 1 + rows, 0:cols, :] = x_ref[...]

    barrier = pltpu.get_barrier_semaphore()

    def greet(dd, hh):
        pl.semaphore_signal(barrier, inc=1, device_id=(dd, hh), device_id_type=MESH)

    def peer(step):
        return ((z + step) % outer) * 2 + x

    greet(other, h)
    for step in range(1, height):
        greet(d, (h + step) % height)
        greet(other, (h + step) % height)

    def greet_line(step, carry):
        greet(peer(step), h)
        return carry

    lax.fori_loop(1, outer, greet_line, 0)
    corners = [(dz, dy) for dz in (-1, 1) for dy in (-1, 1)]
    ways = [(dz, 0) for dz in (-1, 1)] + [(0, dy) for dy in (-1, 1)] + corners

    def exists(dz, dy):
        found = None
        for delta, place, extent in ((dz, d, depth), (dy, h, height)):
            if delta:
                here = (place + delta >= 0) & (place + delta < extent)
                found = here if found is None else found & here
        return found

    count = 1 + 2 * (height - 1) + (outer - 1)
    for dz, dy in ways:
        if dz == 0:
            continue
        there = exists(dz, dy)
        count = count + jnp.where(there, 1, 0)

        @pl.when(there)
        def _(dz=dz, dy=dy):
            greet(d + dz, h + dy)

    pl.semaphore_wait(barrier, count)

    def span(delta, extent, receiving):
        if delta == 0:
            return pl.ds(1, extent)
        if receiving:
            return pl.ds(0 if delta > 0 else extent + 1, 1)
        return pl.ds(extent if delta > 0 else 1, 1)

    def halo_copy(index, dz, dy):
        return pltpu.make_async_remote_copy(
            src_ref=halo.at[span(dz, planes, False), span(dy, rows, False)],
            dst_ref=halo.at[span(dz, planes, True), span(dy, rows, True)],
            send_sem=halo_send.at[index],
            recv_sem=halo_recv.at[index],
            device_id=(d + dz, h + dy),
            device_id_type=MESH,
        )

    def pair_copy(source, target, send_sem, recv_sem):
        return pltpu.make_async_remote_copy(
            src_ref=source,
            dst_ref=target,
            send_sem=send_sem,
            recv_sem=recv_sem,
            device_id=(other, h),
            device_id_type=MESH,
        )

    def swap_copy(array):
        return pair_copy(
            sources[array], swapped.at[array], swap_send.at[array], swap_recv.at[array]
        )

    sources = {KEYS: k_ref, VALUES: v_ref, QUERIES: q_ref}
    swap_copy(KEYS).start()
    for index, (dz, dy) in enumerate(ways):
        @pl.when(exists(dz, dy))
        def _(index=index, dz=dz, dy=dy):
            halo_copy(index, dz, dy).start()
    swap_copy(VALUES).start()
    swap_copy(QUERIES).start()

    lane = lax.broadcasted_iota(jnp.int32, (tokens, width), 1)
    tall_lane = lax.broadcasted_iota(jnp.int32, (2 * tokens, width), 1)
    halves = [lane < HSZ, lane >= HSZ]
    tall_halves = [tall_lane < HSZ, tall_lane >= HSZ]
    mine = (lane >= x * HSZ) & (lane < (x + 1) * HSZ)

    def turned(value):
        return pltpu.roll(value, HSZ, 1)

    def merged(own, received):
        return jnp.where(mine, own.astype(F32), turned(received.astype(F32))).astype(BF)

    def block_copy(array, step):
        return pltpu.make_async_remote_copy(
            src_ref=blocks.at[array, z],
            dst_ref=blocks.at[array, z],
            send_sem=own_send.at[array, step],
            recv_sem=block_recv.at[array, z],
            device_id=(peer(step), h),
            device_id_type=MESH,
        )

    def block_wait(array, slot):
        pltpu.make_async_remote_copy(
            src_ref=blocks.at[array, slot],
            dst_ref=blocks.at[array, slot],
            send_sem=own_send.at[array, 0],
            recv_sem=block_recv.at[array, slot],
            device_id=(other, h),
            device_id_type=MESH,
        ).wait_recv()

    def send_own(array):
        def one(step, carry):
            block_copy(array, step).start()
            return carry
        lax.fori_loop(1, outer, one, 0)

    def wait_all(array):
        def one(step, carry):
            block_wait(array, (z + step) % outer)
            return carry
        lax.fori_loop(1, outer, one, 0)

    load_d.wait()
    features = d_raw.shape[0]
    part_len = d_tall.shape[1] // 8
    for start in range(0, features, part_len):
        wide = d_raw[start : start + part_len].astype(F32).reshape(part_len * 8, channels)
        for lanes in range(d_tall.shape[0]):
            d_tall[lanes] = wide[:, lanes * 128 : (lanes + 1) * 128]
        for s in range(8):
            for lanes in range(d_tall.shape[0]):
                d_ref[s, start : start + part_len, lanes * 128 : (lanes + 1) * 128] = d_tall[
                    lanes, pl.ds(s, part_len, stride=8), :
                ].astype(BF)

    for array in (KEYS, VALUES, QUERIES):
        swap_copy(array).wait_recv()
        blocks[array, z] = merged(sources[array][...], swapped[array])
        send_own(array)

    for index, (dz, dy) in enumerate(ways):
        @pl.when(exists(-dz, -dy))
        def _(index=index, dz=dz, dy=dy):
            halo_copy(index, dz, dy).wait_recv()
    load_w.wait()
    flat = planes * rows * colp
    total = None
    for l in range(3):
        part = None
        for i in range(3):
            for j in range(3):
                window = halo[2 - i : 2 - i + planes, 2 - j : 2 - j + rows].reshape(flat, channels)
                term = dot_nt(window, w_ref[i, j, l])
                part = term if part is None else part + term
        if l != 1:
            part = pltpu.roll(part, (flat - 1) if l == 0 else 1, 0)
        total = part if total is None else total + part
    voxels[...] = (LOSS_SCALE * total).astype(BF).reshape(planes, rows, colp, channels)

    total = None
    for c in range(2):
        part = None
        for a in range(2):
            for b in range(2):
                lhs = jnp.concatenate([voxels[a, 2 * t + b] for t in range(tok_rows)], axis=0)
                term = dot_nt(lhs, d_ref[4 * a + 2 * b + c])
                part = term if part is None else part + term
        if c == 1:
            part = pltpu.roll(part, tok_rows * colp - 1, 0)
        total = part if total is None else total + part
    pick = selection(
        (tokp, tok_rows * colp), [(t * tok_cols, tok_cols, t * colp, 2) for t in range(tok_rows)]
    )
    compact = dot_nn(pick, total.astype(BF)).astype(BF)
    for hh in range(height):
        pieces[hh] = compact[:, hh * width : (hh + 1) * width]

    def piece_copy(away, step):
        target = (h + step) % height
        return pltpu.make_async_remote_copy(
            src_ref=pieces.at[target],
            dst_ref=landed.at[away, h],
            send_sem=piece_send.at[away, step],
            recv_sem=piece_recv.at[away, h],
            device_id=(other if away else d, target),
            device_id_type=MESH,
        )

    def piece_wait(away, slot):
        pltpu.make_async_remote_copy(
            src_ref=landed.at[away, slot],
            dst_ref=landed.at[away, slot],
            send_sem=piece_send.at[away, 0],
            recv_sem=piece_recv.at[away, slot],
            device_id=(other, h),
            device_id_type=MESH,
        ).wait_recv()

    for step in range(height):
        if step:
            piece_copy(0, step).start()
        piece_copy(1, step).start()
    landed[0, h] = pieces[h]

    def placed(block):
        wide = block.astype(F32)
        low = [jnp.where(half, wide, 0.0) for half in halves]
        return [
            jnp.concatenate([low[0], turned(low[1])], axis=0).astype(BF),
            jnp.concatenate([turned(low[0]), low[1]], axis=0).astype(BF),
        ]

    def joined():
        return acc[0] + turned(acc[1])

    def clear(which):
        for f in range(2):
            which[f] = jnp.zeros((2 * tokens, width), F32)

    q_rows = [(part.astype(F32) * scale).astype(BF) for part in placed(blocks[QUERIES, z])]

    for step in range(1, height):
        piece_wait(0, (h + step) % height)
    for step in range(height):
        piece_wait(1, (h + step) % height)
    spread = selection((tokens, height * tokp), [(s * toks, toks, s * tokp, 1) for s in range(height)])
    near, far = [
        dot_nn(spread, landed[away].reshape(height * tokp, width)) for away in range(2)
    ]
    blocks[GRADS, z] = jnp.where(mine, near, turned(far)).astype(BF)
    send_own(GRADS)
    g_rows = placed(blocks[GRADS, z])

    def max_step(step, carry):
        slot = (z + step) % outer

        @pl.when(step > 0)
        def _():
            block_wait(KEYS, slot)

        keys = blocks[KEYS, slot]
        return jnp.maximum(carry, jnp.maximum(dot_nt(q_rows[0], keys), dot_nt(q_rows[1], keys)))

    top = lax.fori_loop(0, outer, max_step, jnp.full((2 * tokens, tokens), -1e30, F32))
    top = jnp.max(top, axis=1, keepdims=True)
    clear(acc)

    def sum_step(step, carry):
        slot = (z + step) % outer

        @pl.when(step > 0)
        def _():
            block_wait(VALUES, slot)

        keys = blocks[KEYS, slot]
        values = blocks[VALUES, slot].astype(F32)
        for f in range(2):
            weights = jnp.exp(dot_nt(q_rows[f], keys) - top).astype(BF)
            probs[slot, f] = weights
            acc[f] += dot_nn(weights, jnp.where(halves[f], values, 1.0).astype(BF))
        return carry

    lax.fori_loop(0, outer, sum_step, 0)
    both = joined()
    sums = turned(both)[:, 0:1]
    inverse = 1.0 / sums
    product = jnp.where(tall_halves[0], both * inverse, 0.0) * g_rows[0].astype(F32)
    delta = jnp.sum(product, axis=1, keepdims=True)
    norm = top + jnp.log(sums)
    columns = [norm[:tokens], norm[tokens:], delta[:tokens], delta[tokens:]]
    table = jnp.zeros((tokens, width), F32)
    for n, column in enumerate(columns):
        table = jnp.where(lane == n, column, table)
    padded = stats.shape[2]
    if padded > tokens:
        table = jnp.concatenate([table, jnp.zeros((padded - tokens, width), F32)], axis=0)
    stats[z] = table.T[: stats.shape[1]]

    def stat_copy(step):
        return pltpu.make_async_remote_copy(
            src_ref=stats.at[z],
            dst_ref=stats.at[z],
            send_sem=stat_send.at[step],
            recv_sem=stat_recv.at[z],
            device_id=(peer(step), h),
            device_id_type=MESH,
        )

    def stat_wait(slot):
        pltpu.make_async_remote_copy(
            src_ref=stats.at[slot],
            dst_ref=stats.at[slot],
            send_sem=stat_send.at[0],
            recv_sem=stat_recv.at[slot],
            device_id=(other, h),
            device_id_type=MESH,
        ).wait_recv()

    def stat_start(step, carry):
        stat_copy(step).start()
        return carry

    lax.fori_loop(1, outer, stat_start, 0)

    def return_copy(index):
        return pair_copy(
            results.at[index], returned.at[index], return_send.at[index], return_recv.at[index]
        )

    def give_back(index, value):
        results[index] = jnp.where(halves[0], value[:tokens], turned(value[tokens:])).astype(BF)
        return_copy(index).start()

    clear(acc)

    def query_step(slot, carry):
        keys = blocks[KEYS, slot]
        values = blocks[VALUES, slot]
        for f in range(2):
            slopes = dot_nt(g_rows[f], values)
            score = (probs[slot, f].astype(F32) * (slopes - delta)).astype(BF)
            acc[f] += dot_nn(score, keys)
        return carry

    lax.fori_loop(0, outer, query_step, 0)
    give_back(0, joined() * (inverse * scale))

    k_rows = [(part.astype(F32) * scale).astype(BF) for part in placed(blocks[KEYS, z])]
    v_rows = placed(blocks[VALUES, z])
    for n in range(4):
        acc[n] = jnp.zeros((2 * tokens, width), F32)

    def owner_step(step, carry):
        slot = (z + step) % outer

        @pl.when(step > 0)
        def _():
            block_wait(QUERIES, slot)
            stat_wait(slot)
            block_wait(GRADS, slot)

        queries = blocks[QUERIES, slot]
        grads = blocks[GRADS, slot]
        table = stats[slot]
        for f in range(2):
            weights = jnp.exp(dot_nt(k_rows[f], queries) - table[f : f + 1, :tokens])
            slopes = dot_nt(v_rows[f], grads) - table[2 + f : 3 + f, :tokens]
            acc[f] += dot_nn((weights * slopes).astype(BF), queries)
            acc[2 + f] += dot_nn(weights.astype(BF), grads)
        return carry

    lax.fori_loop(0, outer, owner_step, 0)
    give_back(1, joined() * scale)
    give_back(2, acc[2] + turned(acc[3]))
    for index, out in enumerate((dq_ref, dk_ref, dv_ref)):
        return_copy(index).wait_recv()
        out[...] = merged(results[index], returned[index])

    for index in range(3):
        return_copy(index).wait_send()
        swap_copy(index).wait_send()
    for index, (dz, dy) in enumerate(ways):
        @pl.when(exists(dz, dy))
        def _(index=index, dz=dz, dy=dy):
            halo_copy(index, dz, dy).wait_send()
    for step in range(height):
        if step:
            piece_copy(0, step).wait_send()
        piece_copy(1, step).wait_send()

    def drain(step, carry):
        for array in range(4):
            block_copy(array, step).wait_send()
        stat_copy(step).wait_send()
        return carry

    lax.fori_loop(1, outer, drain, 0)


def hand_over(a_ref, b_ref, c_ref, a_out, b_out, c_out):
    a_out[...] = a_ref[...]
    b_out[...] = b_ref[...]
    c_out[...] = c_ref[...]


def body(mesh_sizes, queries, key_vectors, value_vectors, grad_conv, conv_weight, dec_weight):
    depth, height = mesh_sizes
    outer = depth // 2
    planes, rows, cols, channels = grad_conv.shape
    colp = round_up(cols + 1, 16)
    tokens, width = queries.shape
    assert depth % 2 == 0 and width == 2 * HSZ
    tokp = round_up((rows // 2) * (cols // 2), 16)
    features = dec_weight.shape[0]
    out = jax.ShapeDtypeStruct((tokens, width), BF)
    vmem = pl.BlockSpec(memory_space=pltpu.VMEM)
    hbm = pl.BlockSpec(memory_space=pl.ANY)
    dma = pltpu.SemaphoreType.DMA
    results = pl.pallas_call(
        functools.partial(kernel, depth, height),
        out_shape=(out, out, out),
        in_specs=[vmem, vmem, vmem, vmem, hbm, hbm],
        out_specs=(vmem, vmem, vmem),
        scratch_shapes=[
            pltpu.VMEM((planes + 2, rows + 2, colp, channels), BF),
            pltpu.VMEM(conv_weight.shape, BF),
            pltpu.VMEM(dec_weight.shape, BF),
            pltpu.VMEM((channels // 128, 512, 128), F32),
            pltpu.VMEM((8, features, channels), BF),
            pltpu.VMEM((planes, rows, colp, channels), BF),
            pltpu.VMEM((height, tokp, width), BF),
            pltpu.VMEM((2, height, tokp, width), BF),
            pltpu.VMEM((3, tokens, width), BF),
            pltpu.VMEM((4, outer, tokens, width), BF),
            pltpu.VMEM((outer, 8, round_up(tokens, 128)), F32),
            pltpu.VMEM((outer, 2, 2 * tokens, tokens), BF),
            pltpu.VMEM((4, 2 * tokens, width), F32),
            pltpu.VMEM((3, tokens, width), BF),
            pltpu.VMEM((3, tokens, width), BF),
            dma((2,)),
            dma((8,)),
            dma((8,)),
            dma((2, height)),
            dma((2, height)),
            dma((3,)),
            dma((3,)),
            dma((4, outer)),
            dma((4, outer)),
            dma((outer,)),
            dma((outer,)),
            dma((3,)),
            dma((3,)),
        ],
        compiler_params=pltpu.CompilerParams(
            collective_id=0, has_side_effects=True, vmem_limit_bytes=58 * 2**20
        ),
        cost_estimate=pl.CostEstimate(
            flops=4 * 10**9, bytes_accessed=8 * 10**6, transcendentals=2 * 10**6
        ),
    )(queries, key_vectors, value_vectors, grad_conv, conv_weight, dec_weight)
    return pl.pallas_call(
        hand_over,
        out_shape=(out, out, out),
        in_specs=[vmem, vmem, vmem],
        out_specs=(vmem, vmem, vmem),
    )(*results)


def solution(mesh):
    in_specs = (
        P("depth", "height"),
        P("depth", "height"),
        P("depth", "height"),
        P("depth", "height", None, None),
        P(),
        P(),
    )
    out_specs = (P("depth", "height"), P("depth", "height"), P("depth", "height"))
    sizes = (mesh.shape["depth"], mesh.shape["height"])
    return jax.shard_map(
        functools.partial(body, sizes),
        mesh=mesh,
        in_specs=in_specs,
        out_specs=out_specs,
        check_vma=False,
    )
```

```python
import functools
import math

import jax
import jax.numpy as jnp
from jax import lax
from jax.experimental import pallas as pl
from jax.experimental.pallas import tpu as pltpu
from jax.sharding import PartitionSpec as P

HSZ = 64
LOSS_SCALE = 64.0
MESH = pl.DeviceIdType.MESH
BF = jnp.bfloat16
F32 = jnp.float32
KEYS, VALUES, QUERIES, GRADS = range(4)


def round_up(value, multiple):
    return (value + multiple - 1) // multiple * multiple


def dot_nt(left, right):
    return lax.dot_general(left, right, (((1,), (1,)), ((), ())), preferred_element_type=F32)


def dot_nn(left, right):
    return lax.dot_general(left, right, (((1,), (0,)), ((), ())), preferred_element_type=F32)


def selection(shape, runs):
    row = lax.broadcasted_iota(jnp.int32, shape, 0)
    col = lax.broadcasted_iota(jnp.int32, shape, 1)
    chosen = None
    for first, count, start, step in runs:
        hit = (row >= first) & (row < first + count) & (col == start + step * (row - first))
        chosen = hit if chosen is None else chosen | hit
    return chosen.astype(F32).astype(BF)


def kernel(
    depth, height,
    q_ref, k_ref, v_ref, x_ref, w_hbm, d_hbm,
    dq_ref, dk_ref, dv_ref,
    halo, w_ref, d_raw, d_tall, d_ref, windows, voxels, pieces, landed, swapped, blocks, stats, probs,
    acc, results, returned,
    load_sems, halo_send, halo_recv, piece_send, piece_recv, swap_send, swap_recv,
    own_send, block_recv, stat_send, stat_recv, return_send, return_recv,
):
    planes, rows, cols, channels = x_ref.shape
    colp = halo.shape[2]
    tokens, width = q_ref.shape
    scale = 1.0 / math.sqrt(HSZ)
    outer = depth // 2
    groups, chunk = probs.shape[0], outer // probs.shape[0]
    tok_rows, tok_cols = rows // 2, cols // 2
    toks = tok_rows * tok_cols
    tokp = pieces.shape[1]

    d = lax.axis_index("depth")
    h = lax.axis_index("height")
    z, x = d // 2, d % 2
    other = 2 * z + (1 - x)

    taps = [(i, j) for i in range(3) for j in range(3)]
    load_d = pltpu.make_async_copy(d_hbm, d_raw, load_sems.at[27])
    load_d.start()
    loads_w = []
    for n, (i, j) in enumerate(taps):
        for l in range(3):
            loads_w.append(
                pltpu.make_async_copy(
                    w_hbm.at[i, j, l],
                    w_ref.at[pl.ds(l * channels, channels), pl.ds(n * channels, channels)],
                    load_sems.at[3 * n + l],
                )
            )
    for load in loads_w:
        load.start()

    halo[...] = jnp.zeros_like(halo)
    halo[1 : 1 + planes, 1 : 1 + rows, 0:cols, :] = x_ref[...]

    barrier = pltpu.get_barrier_semaphore()

    def greet(dd, hh):
        pl.semaphore_signal(barrier, inc=1, device_id=(dd, hh), device_id_type=MESH)

    def peer(step):
        return ((z + step) % outer) * 2 + x

    greet(other, h)
    for step in range(1, height):
        greet(d, (h + step) % height)
        greet(other, (h + step) % height)

    def greet_line(step, carry):
        greet(peer(step), h)
        return carry

    lax.fori_loop(1, outer, greet_line, 0)
    corners = [(dz, dy) for dz in (-1, 1) for dy in (-1, 1)]
    ways = [(dz, 0) for dz in (-1, 1)] + [(0, dy) for dy in (-1, 1)] + corners

    def exists(dz, dy):
        found = None
        for delta, place, extent in ((dz, d, depth), (dy, h, height)):
            if delta:
                here = (place + delta >= 0) & (place + delta < extent)
                found = here if found is None else found & here
        return found

    count = 1 + 2 * (height - 1) + (outer - 1)
    for dz, dy in ways:
        if dz == 0:
            continue
        there = exists(dz, dy)
        count = count + jnp.where(there, 1, 0)

        @pl.when(there)
        def _(dz=dz, dy=dy):
            greet(d + dz, h + dy)

    pl.semaphore_wait(barrier, count)

    def span(delta, extent, receiving):
        if delta == 0:
            return pl.ds(1, extent)
        if receiving:
            return pl.ds(0 if delta > 0 else extent + 1, 1)
        return pl.ds(extent if delta > 0 else 1, 1)

    def halo_copy(index, dz, dy):
        return pltpu.make_async_remote_copy(
            src_ref=halo.at[span(dz, planes, False), span(dy, rows, False)],
            dst_ref=halo.at[span(dz, planes, True), span(dy, rows, True)],
            send_sem=halo_send.at[index],
            recv_sem=halo_recv.at[index],
            device_id=(d + dz, h + dy),
            device_id_type=MESH,
        )

    def pair_copy(source, target, send_sem, recv_sem):
        return pltpu.make_async_remote_copy(
            src_ref=source,
            dst_ref=target,
            send_sem=send_sem,
            recv_sem=recv_sem,
            device_id=(other, h),
            device_id_type=MESH,
        )

    def swap_copy(array):
        return pair_copy(
            sources[array], swapped.at[array], swap_send.at[array], swap_recv.at[array]
        )

    sources = {KEYS: k_ref, VALUES: v_ref, QUERIES: q_ref}
    swap_copy(KEYS).start()
    for index, (dz, dy) in enumerate(ways):
        @pl.when(exists(dz, dy))
        def _(index=index, dz=dz, dy=dy):
            halo_copy(index, dz, dy).start()
    swap_copy(VALUES).start()
    swap_copy(QUERIES).start()

    lane = lax.broadcasted_iota(jnp.int32, (tokens, width), 1)
    tall_lane = lax.broadcasted_iota(jnp.int32, (2 * tokens, width), 1)
    halves = [lane < HSZ, lane >= HSZ]
    tall_halves = [tall_lane < HSZ, tall_lane >= HSZ]
    mine = (lane >= x * HSZ) & (lane < (x + 1) * HSZ)

    def turned(value):
        return pltpu.roll(value, HSZ, 1)

    def merged(own, received):
        return jnp.where(mine, own.astype(F32), turned(received.astype(F32))).astype(BF)

    def block_copy(array, step):
        return pltpu.make_async_remote_copy(
            src_ref=blocks.at[array, z],
            dst_ref=blocks.at[array, z],
            send_sem=own_send.at[array, step],
            recv_sem=block_recv.at[array, z],
            device_id=(peer(step), h),
            device_id_type=MESH,
        )

    def block_wait(array, slot):
        pltpu.make_async_remote_copy(
            src_ref=blocks.at[array, slot],
            dst_ref=blocks.at[array, slot],
            send_sem=own_send.at[array, 0],
            recv_sem=block_recv.at[array, slot],
            device_id=(other, h),
            device_id_type=MESH,
        ).wait_recv()

    def send_own(array):
        def one(step, carry):
            block_copy(array, step).start()
            return carry
        lax.fori_loop(1, outer, one, 0)

    def wait_all(array):
        def one(step, carry):
            block_wait(array, (z + step) % outer)
            return carry
        lax.fori_loop(1, outer, one, 0)

    load_d.wait()
    features = d_raw.shape[0]
    part_len = d_tall.shape[1] // 8
    for start in range(0, features, part_len):
        wide = d_raw[start : start + part_len].astype(F32).reshape(part_len * 8, channels)
        for lanes in range(d_tall.shape[0]):
            d_tall[lanes] = wide[:, lanes * 128 : (lanes + 1) * 128]
        for s in range(8):
            for lanes in range(d_tall.shape[0]):
                place = (s // 2) * channels + lanes * 128
                d_ref[s % 2, start : start + part_len, place : place + 128] = d_tall[
                    lanes, pl.ds(s, part_len, stride=8), :
                ].astype(BF)

    for array in (KEYS, VALUES, QUERIES):
        swap_copy(array).wait_recv()
        blocks[array, z] = merged(sources[array][...], swapped[array])
        send_own(array)

    for index, (dz, dy) in enumerate(ways):
        @pl.when(exists(-dz, -dy))
        def _(index=index, dz=dz, dy=dy):
            halo_copy(index, dz, dy).wait_recv()
    for load in loads_w:
        load.wait()
    flat = planes * rows * colp
    for n, (i, j) in enumerate(taps):
        window = halo[2 - i : 2 - i + planes, 2 - j : 2 - j + rows]
        windows[:, n * channels : (n + 1) * channels] = window.reshape(flat, channels)
    sums = dot_nt(windows[...], w_ref[...])
    total = (
        pltpu.roll(sums[:, :channels], flat - 1, 0)
        + sums[:, channels : 2 * channels]
        + pltpu.roll(sums[:, 2 * channels :], 1, 0)
    )
    voxels[...] = (LOSS_SCALE * total).astype(BF).reshape(planes, rows, colp, channels)

    lhs = jnp.concatenate(
        [
            jnp.concatenate([voxels[a, 2 * t + b] for t in range(tok_rows)], axis=0)
            for a in range(2)
            for b in range(2)
        ],
        axis=1,
    )
    parts = [dot_nt(lhs, d_ref[c]) for c in range(2)]
    total = parts[0] + pltpu.roll(parts[1], tok_rows * colp - 1, 0)
    pick = selection(
        (tokp, tok_rows * colp), [(t * tok_cols, tok_cols, t * colp, 2) for t in range(tok_rows)]
    )
    compact = dot_nn(pick, total.astype(BF)).astype(BF)
    for hh in range(height):
        pieces[hh] = compact[:, hh * width : (hh + 1) * width]

    def piece_copy(away, step):
        target = (h + step) % height
        return pltpu.make_async_remote_copy(
            src_ref=pieces.at[target],
            dst_ref=landed.at[away, h],
            send_sem=piece_send.at[away, step],
            recv_sem=piece_recv.at[away, h],
            device_id=(other if away else d, target),
            device_id_type=MESH,
        )

    def piece_wait(away, slot):
        pltpu.make_async_remote_copy(
            src_ref=landed.at[away, slot],
            dst_ref=landed.at[away, slot],
            send_sem=piece_send.at[away, 0],
            recv_sem=piece_recv.at[away, slot],
            device_id=(other, h),
            device_id_type=MESH,
        ).wait_recv()

    for step in range(height):
        if step:
            piece_copy(0, step).start()
        piece_copy(1, step).start()
    landed[0, h] = pieces[h]

    def placed(block):
        wide = block.astype(F32)
        low = [jnp.where(half, wide, 0.0) for half in halves]
        return [
            jnp.concatenate([low[0], turned(low[1])], axis=0).astype(BF),
            jnp.concatenate([turned(low[0]), low[1]], axis=0).astype(BF),
        ]

    def joined():
        return acc[0] + turned(acc[1])

    def clear(which):
        for f in range(2):
            which[f] = jnp.zeros((2 * tokens, width), F32)

    q_rows = [(part.astype(F32) * scale).astype(BF) for part in placed(blocks[QUERIES, z])]

    for step in range(1, height):
        piece_wait(0, (h + step) % height)
    for step in range(height):
        piece_wait(1, (h + step) % height)
    spread = selection((tokens, height * tokp), [(s * toks, toks, s * tokp, 1) for s in range(height)])
    near, far = [
        dot_nn(spread, landed[away].reshape(height * tokp, width)) for away in range(2)
    ]
    blocks[GRADS, z] = jnp.where(mine, near, turned(far)).astype(BF)
    send_own(GRADS)
    g_rows = placed(blocks[GRADS, z])

    def span_of(array, group):
        part = blocks[array, pl.ds(group * chunk, chunk)]
        return part.reshape(chunk * tokens, width)

    def logits(group):
        keys = span_of(KEYS, group)
        return [dot_nt(q_rows[f], keys) for f in range(2)]

    def highest(values):
        return jnp.max(jnp.maximum(values[0], values[1]), axis=1, keepdims=True)

    long_lane = lax.broadcasted_iota(jnp.int32, (chunk * tokens, width), 1)
    long_halves = [long_lane < HSZ, long_lane >= HSZ]

    def accumulate(group, values, first):
        held = span_of(VALUES, group).astype(F32)
        for f in range(2):
            weights = jnp.exp(values[f] - top).astype(BF)
            probs[group, f] = weights
            term = dot_nn(weights, jnp.where(long_halves[f], held, 1.0).astype(BF))
            acc[f] = term if first else acc[f] + term

    wait_all(KEYS)
    if groups == 1:
        values = logits(0)
        top = highest(values)
        wait_all(VALUES)
        accumulate(0, values, True)
    else:
        def max_step(group, carry):
            return jnp.maximum(carry, highest(logits(group)))

        top = lax.fori_loop(0, groups, max_step, jnp.full((2 * tokens, 1), -1e30, F32))
        wait_all(VALUES)
        clear(acc)

        def sum_step(group, carry):
            accumulate(group, logits(group), False)
            return carry

        lax.fori_loop(0, groups, sum_step, 0)
    both = joined()
    sums = turned(both)[:, 0:1]
    inverse = 1.0 / sums
    product = jnp.where(tall_halves[0], both * inverse, 0.0) * g_rows[0].astype(F32)
    delta = jnp.sum(product, axis=1, keepdims=True)
    norm = top + jnp.log(sums)
    columns = [norm[:tokens], norm[tokens:], delta[:tokens], delta[tokens:]]
    table = jnp.zeros((tokens, width), F32)
    for n, column in enumerate(columns):
        table = jnp.where(lane == n, column, table)
    padded = stats.shape[2]
    if padded > tokens:
        table = jnp.concatenate([table, jnp.zeros((padded - tokens, width), F32)], axis=0)
    stats[z] = table.T[: stats.shape[1]]

    def stat_copy(step):
        return pltpu.make_async_remote_copy(
            src_ref=stats.at[z],
            dst_ref=stats.at[z],
            send_sem=stat_send.at[step],
            recv_sem=stat_recv.at[z],
            device_id=(peer(step), h),
            device_id_type=MESH,
        )

    def stat_wait(slot):
        pltpu.make_async_remote_copy(
            src_ref=stats.at[slot],
            dst_ref=stats.at[slot],
            send_sem=stat_send.at[0],
            recv_sem=stat_recv.at[slot],
            device_id=(other, h),
            device_id_type=MESH,
        ).wait_recv()

    def stat_start(step, carry):
        stat_copy(step).start()
        return carry

    lax.fori_loop(1, outer, stat_start, 0)

    def return_copy(index):
        return pair_copy(
            results.at[index], returned.at[index], return_send.at[index], return_recv.at[index]
        )

    def give_back(index, value):
        results[index] = jnp.where(halves[0], value[:tokens], turned(value[tokens:])).astype(BF)
        return_copy(index).start()

    def query_block(group, first):
        keys = span_of(KEYS, group)
        held = span_of(VALUES, group)
        for f in range(2):
            slopes = dot_nt(g_rows[f], held)
            score = (probs[group, f].astype(F32) * (slopes - delta)).astype(BF)
            term = dot_nn(score, keys)
            acc[f] = term if first else acc[f] + term

    if groups == 1:
        query_block(0, True)
    else:
        clear(acc)

        def query_step(group, carry):
            query_block(group, False)
            return carry

        lax.fori_loop(0, groups, query_step, 0)
    give_back(0, joined() * (inverse * scale))

    k_rows = [(part.astype(F32) * scale).astype(BF) for part in placed(blocks[KEYS, z])]
    v_rows = placed(blocks[VALUES, z])
    for n in range(4):
        acc[n] = jnp.zeros((2 * tokens, width), F32)

    def owner_step(step, carry):
        slot = (z + step) % outer

        @pl.when(step > 0)
        def _():
            block_wait(QUERIES, slot)
            stat_wait(slot)
            block_wait(GRADS, slot)

        queries = blocks[QUERIES, slot]
        grads = blocks[GRADS, slot]
        table = stats[slot]
        for f in range(2):
            weights = jnp.exp(dot_nt(k_rows[f], queries) - table[f : f + 1, :tokens])
            slopes = dot_nt(v_rows[f], grads) - table[2 + f : 3 + f, :tokens]
            acc[f] += dot_nn((weights * slopes).astype(BF), queries)
            acc[2 + f] += dot_nn(weights.astype(BF), grads)
        return carry

    lax.fori_loop(0, outer, owner_step, 0)
    give_back(1, joined() * scale)
    give_back(2, acc[2] + turned(acc[3]))
    for index, out in enumerate((dq_ref, dk_ref, dv_ref)):
        return_copy(index).wait_recv()
        out[...] = merged(results[index], returned[index])

    for index in range(3):
        return_copy(index).wait_send()
        swap_copy(index).wait_send()
    for index, (dz, dy) in enumerate(ways):
        @pl.when(exists(dz, dy))
        def _(index=index, dz=dz, dy=dy):
            halo_copy(index, dz, dy).wait_send()
    for step in range(height):
        if step:
            piece_copy(0, step).wait_send()
        piece_copy(1, step).wait_send()

    def drain(step, carry):
        for array in range(4):
            block_copy(array, step).wait_send()
        stat_copy(step).wait_send()
        return carry

    lax.fori_loop(1, outer, drain, 0)


def hand_over(a_ref, b_ref, c_ref, a_out, b_out, c_out):
    a_out[...] = a_ref[...]
    b_out[...] = b_ref[...]
    c_out[...] = c_ref[...]


def body(mesh_sizes, queries, key_vectors, value_vectors, grad_conv, conv_weight, dec_weight):
    depth, height = mesh_sizes
    outer = depth // 2
    planes, rows, cols, channels = grad_conv.shape
    colp = round_up(cols + 1, 16)
    tokens, width = queries.shape
    assert depth % 2 == 0 and width == 2 * HSZ
    tokp = round_up((rows // 2) * (cols // 2), 16)
    features = dec_weight.shape[0]
    chunk = math.gcd(outer, 4)
    out = jax.ShapeDtypeStruct((tokens, width), BF)
    vmem = pl.BlockSpec(memory_space=pltpu.VMEM)
    hbm = pl.BlockSpec(memory_space=pl.ANY)
    dma = pltpu.SemaphoreType.DMA
    results = pl.pallas_call(
        functools.partial(kernel, depth, height),
        out_shape=(out, out, out),
        in_specs=[vmem, vmem, vmem, vmem, hbm, hbm],
        out_specs=(vmem, vmem, vmem),
        scratch_shapes=[
            pltpu.VMEM((planes + 2, rows + 2, colp, channels), BF),
            pltpu.VMEM((3 * channels, 9 * channels), BF),
            pltpu.VMEM(dec_weight.shape, BF),
            pltpu.VMEM((channels // 128, 512, 128), F32),
            pltpu.VMEM((2, features, 4 * channels), BF),
            pltpu.VMEM((planes * rows * colp, 9 * channels), BF),
            pltpu.VMEM((planes, rows, colp, channels), BF),
            pltpu.VMEM((height, tokp, width), BF),
            pltpu.VMEM((2, height, tokp, width), BF),
            pltpu.VMEM((3, tokens, width), BF),
            pltpu.VMEM((4, outer, tokens, width), BF),
            pltpu.VMEM((outer, 8, round_up(tokens, 128)), F32),
            pltpu.VMEM((outer // chunk, 2, 2 * tokens, chunk * tokens), BF),
            pltpu.VMEM((4, 2 * tokens, width), F32),
            pltpu.VMEM((3, tokens, width), BF),
            pltpu.VMEM((3, tokens, width), BF),
            dma((28,)),
            dma((8,)),
            dma((8,)),
            dma((2, height)),
            dma((2, height)),
            dma((3,)),
            dma((3,)),
            dma((4, outer)),
            dma((4, outer)),
            dma((outer,)),
            dma((outer,)),
            dma((3,)),
            dma((3,)),
        ],
        compiler_params=pltpu.CompilerParams(
            collective_id=0, has_side_effects=True, vmem_limit_bytes=58 * 2**20
        ),
        cost_estimate=pl.CostEstimate(
            flops=4 * 10**9, bytes_accessed=8 * 10**6, transcendentals=2 * 10**6
        ),
    )(queries, key_vectors, value_vectors, grad_conv, conv_weight, dec_weight)
    return pl.pallas_call(
        hand_over,
        out_shape=(out, out, out),
        in_specs=[vmem, vmem, vmem],
        out_specs=(vmem, vmem, vmem),
    )(*results)


def solution(mesh):
    in_specs = (
        P("depth", "height"),
        P("depth", "height"),
        P("depth", "height"),
        P("depth", "height", None, None),
        P(),
        P(),
    )
    out_specs = (P("depth", "height"), P("depth", "height"), P("depth", "height"))
    sizes = (mesh.shape["depth"], mesh.shape["height"])
    return jax.shard_map(
        functools.partial(body, sizes),
        mesh=mesh,
        in_specs=in_specs,
        out_specs=out_specs,
        check_vma=False,
    )
```

```python
import functools
import math

import jax
import jax.numpy as jnp
from jax import lax
from jax.experimental import pallas as pl
from jax.experimental.pallas import tpu as pltpu
from jax.sharding import PartitionSpec as P

HSZ = 64
LOSS_SCALE = 64.0
MESH = pl.DeviceIdType.MESH
BF = jnp.bfloat16
F32 = jnp.float32
KEYS, VALUES, QUERIES, GRADS = range(4)


def round_up(value, multiple):
    return (value + multiple - 1) // multiple * multiple


def dot_nt(left, right):
    return lax.dot_general(left, right, (((1,), (1,)), ((), ())), preferred_element_type=F32)


def dot_nn(left, right):
    return lax.dot_general(left, right, (((1,), (0,)), ((), ())), preferred_element_type=F32)


def selection(shape, runs):
    row = lax.broadcasted_iota(jnp.int32, shape, 0)
    col = lax.broadcasted_iota(jnp.int32, shape, 1)
    chosen = None
    for first, count, start, step in runs:
        hit = (row >= first) & (row < first + count) & (col == start + step * (row - first))
        chosen = hit if chosen is None else chosen | hit
    return chosen.astype(F32).astype(BF)


def kernel(
    depth, height,
    q_ref, k_ref, v_ref, x_ref, w_hbm, d_hbm,
    dq_ref, dk_ref, dv_ref,
    halo, w_ref, d_raw, d_tall, d_ref, windows, voxels, pieces, landed, swapped, blocks, stats, probs,
    acc, results, returned,
    load_sems, halo_send, halo_recv, piece_send, piece_recv, swap_send, swap_recv,
    own_send, block_recv, stat_send, stat_recv, return_send, return_recv,
):
    planes, rows, cols, channels = x_ref.shape
    colp = halo.shape[2]
    tokens, width = q_ref.shape
    scale = 1.0 / math.sqrt(HSZ)
    outer = depth // 2
    groups, chunk = probs.shape[0], outer // probs.shape[0]
    tok_rows, tok_cols = rows // 2, cols // 2
    toks = tok_rows * tok_cols
    tokp = pieces.shape[1]

    d = lax.axis_index("depth")
    h = lax.axis_index("height")
    z, x = d // 2, d % 2
    other = 2 * z + (1 - x)

    taps = [(i, j) for i in range(3) for j in range(3)]
    load_d = pltpu.make_async_copy(d_hbm, d_raw, load_sems.at[27])
    load_d.start()
    loads_w = []
    for n, (i, j) in enumerate(taps):
        for l in range(3):
            loads_w.append(
                pltpu.make_async_copy(
                    w_hbm.at[i, j, l],
                    w_ref.at[pl.ds(l * channels, channels), pl.ds(n * channels, channels)],
                    load_sems.at[3 * n + l],
                )
            )
    for load in loads_w:
        load.start()

    halo[...] = jnp.zeros_like(halo)
    halo[1 : 1 + planes, 1 : 1 + rows, 0:cols, :] = x_ref[...]

    barrier = pltpu.get_barrier_semaphore()

    def greet(dd, hh):
        pl.semaphore_signal(barrier, inc=1, device_id=(dd, hh), device_id_type=MESH)

    def peer(step):
        return ((z + step) % outer) * 2 + x

    greet(other, h)
    for step in range(1, height):
        greet(d, (h + step) % height)
        greet(other, (h + step) % height)

    def greet_line(step, carry):
        greet(peer(step), h)
        return carry

    lax.fori_loop(1, outer, greet_line, 0)
    corners = [(dz, dy) for dz in (-1, 1) for dy in (-1, 1)]
    ways = [(dz, 0) for dz in (-1, 1)] + [(0, dy) for dy in (-1, 1)] + corners

    def exists(dz, dy):
        found = None
        for delta, place, extent in ((dz, d, depth), (dy, h, height)):
            if delta:
                here = (place + delta >= 0) & (place + delta < extent)
                found = here if found is None else found & here
        return found

    count = 1 + 2 * (height - 1) + (outer - 1)
    for dz, dy in ways:
        if dz == 0:
            continue
        there = exists(dz, dy)
        count = count + jnp.where(there, 1, 0)

        @pl.when(there)
        def _(dz=dz, dy=dy):
            greet(d + dz, h + dy)

    pl.semaphore_wait(barrier, count)

    def span(delta, extent, receiving):
        if delta == 0:
            return pl.ds(1, extent)
        if receiving:
            return pl.ds(0 if delta > 0 else extent + 1, 1)
        return pl.ds(extent if delta > 0 else 1, 1)

    def halo_copy(index, dz, dy):
        return pltpu.make_async_remote_copy(
            src_ref=halo.at[span(dz, planes, False), span(dy, rows, False)],
            dst_ref=halo.at[span(dz, planes, True), span(dy, rows, True)],
            send_sem=halo_send.at[index],
            recv_sem=halo_recv.at[index],
            device_id=(d + dz, h + dy),
            device_id_type=MESH,
        )

    def pair_copy(source, target, send_sem, recv_sem):
        return pltpu.make_async_remote_copy(
            src_ref=source,
            dst_ref=target,
            send_sem=send_sem,
            recv_sem=recv_sem,
            device_id=(other, h),
            device_id_type=MESH,
        )

    def swap_copy(array):
        return pair_copy(
            sources[array], swapped.at[array], swap_send.at[array], swap_recv.at[array]
        )

    sources = {KEYS: k_ref, VALUES: v_ref, QUERIES: q_ref}
    for index, (dz, dy) in enumerate(ways):
        @pl.when(exists(dz, dy))
        def _(index=index, dz=dz, dy=dy):
            halo_copy(index, dz, dy).start()
    for array in (KEYS, VALUES, QUERIES):
        swap_copy(array).start()

    lane = lax.broadcasted_iota(jnp.int32, (tokens, width), 1)
    tall_lane = lax.broadcasted_iota(jnp.int32, (2 * tokens, width), 1)
    halves = [lane < HSZ, lane >= HSZ]
    tall_halves = [tall_lane < HSZ, tall_lane >= HSZ]
    mine = (lane >= x * HSZ) & (lane < (x + 1) * HSZ)

    def turned(value):
        return pltpu.roll(value, HSZ, 1)

    def merged(own, received):
        return jnp.where(mine, own.astype(F32), turned(received.astype(F32))).astype(BF)

    def block_copy(array, step):
        return pltpu.make_async_remote_copy(
            src_ref=blocks.at[array, z],
            dst_ref=blocks.at[array, z],
            send_sem=own_send.at[array, step],
            recv_sem=block_recv.at[array, z],
            device_id=(peer(step), h),
            device_id_type=MESH,
        )

    def block_wait(array, slot):
        pltpu.make_async_remote_copy(
            src_ref=blocks.at[array, slot],
            dst_ref=blocks.at[array, slot],
            send_sem=own_send.at[array, 0],
            recv_sem=block_recv.at[array, slot],
            device_id=(other, h),
            device_id_type=MESH,
        ).wait_recv()

    def send_own(array):
        def one(step, carry):
            block_copy(array, step).start()
            return carry
        lax.fori_loop(1, outer, one, 0)

    def wait_all(array):
        def one(step, carry):
            block_wait(array, (z + step) % outer)
            return carry
        lax.fori_loop(1, outer, one, 0)

    load_d.wait()
    features = d_raw.shape[0]
    part_len = d_tall.shape[1] // 8
    for start in range(0, features, part_len):
        wide = d_raw[start : start + part_len].astype(F32).reshape(part_len * 8, channels)
        for lanes in range(d_tall.shape[0]):
            d_tall[lanes] = wide[:, lanes * 128 : (lanes + 1) * 128]
        for s in range(8):
            for lanes in range(d_tall.shape[0]):
                place = (s // 2) * channels + lanes * 128
                d_ref[s % 2, start : start + part_len, place : place + 128] = d_tall[
                    lanes, pl.ds(s, part_len, stride=8), :
                ].astype(BF)

    def pass_on(array):
        swap_copy(array).wait_recv()
        blocks[array, z] = merged(sources[array][...], swapped[array])
        send_own(array)

    for index, (dz, dy) in enumerate(ways):
        @pl.when(exists(-dz, -dy))
        def _(index=index, dz=dz, dy=dy):
            halo_copy(index, dz, dy).wait_recv()
    for load in loads_w:
        load.wait()
    flat = planes * rows * colp
    for n, (i, j) in enumerate(taps):
        window = halo[2 - i : 2 - i + planes, 2 - j : 2 - j + rows]
        windows[:, n * channels : (n + 1) * channels] = window.reshape(flat, channels)
    pass_on(KEYS)
    shifts = (flat - 1, 0, 1)
    for l, array in enumerate((VALUES, QUERIES, None)):
        part = dot_nt(windows[...], w_ref[l * channels : (l + 1) * channels])
        if shifts[l]:
            part = pltpu.roll(part, shifts[l], 0)
        total = part if l == 0 else total + part
        if array is not None:
            pass_on(array)
    voxels[...] = (LOSS_SCALE * total).astype(BF).reshape(planes, rows, colp, channels)

    lhs = jnp.concatenate(
        [
            jnp.concatenate([voxels[a, 2 * t + b] for t in range(tok_rows)], axis=0)
            for a in range(2)
            for b in range(2)
        ],
        axis=1,
    )
    parts = [dot_nt(lhs, d_ref[c]) for c in range(2)]
    total = parts[0] + pltpu.roll(parts[1], tok_rows * colp - 1, 0)
    pick = selection(
        (tokp, tok_rows * colp), [(t * tok_cols, tok_cols, t * colp, 2) for t in range(tok_rows)]
    )
    compact = dot_nn(pick, total.astype(BF)).astype(BF)
    for hh in range(height):
        pieces[hh] = compact[:, hh * width : (hh + 1) * width]

    def piece_copy(away, step):
        target = (h + step) % height
        return pltpu.make_async_remote_copy(
            src_ref=pieces.at[target],
            dst_ref=landed.at[away, h],
            send_sem=piece_send.at[away, step],
            recv_sem=piece_recv.at[away, h],
            device_id=(other if away else d, target),
            device_id_type=MESH,
        )

    def piece_wait(away, slot):
        pltpu.make_async_remote_copy(
            src_ref=landed.at[away, slot],
            dst_ref=landed.at[away, slot],
            send_sem=piece_send.at[away, 0],
            recv_sem=piece_recv.at[away, slot],
            device_id=(other, h),
            device_id_type=MESH,
        ).wait_recv()

    for step in range(height):
        if step:
            piece_copy(0, step).start()
        piece_copy(1, step).start()
    landed[0, h] = pieces[h]

    def placed(block):
        wide = block.astype(F32)
        low = [jnp.where(half, wide, 0.0) for half in halves]
        return [
            jnp.concatenate([low[0], turned(low[1])], axis=0).astype(BF),
            jnp.concatenate([turned(low[0]), low[1]], axis=0).astype(BF),
        ]

    def joined():
        return acc[0] + turned(acc[1])

    def clear(which):
        for f in range(2):
            which[f] = jnp.zeros((2 * tokens, width), F32)

    q_rows = [(part.astype(F32) * scale).astype(BF) for part in placed(blocks[QUERIES, z])]

    for step in range(1, height):
        piece_wait(0, (h + step) % height)
    for step in range(height):
        piece_wait(1, (h + step) % height)
    spread = selection((tokens, height * tokp), [(s * toks, toks, s * tokp, 1) for s in range(height)])
    near, far = [
        dot_nn(spread, landed[away].reshape(height * tokp, width)) for away in range(2)
    ]
    blocks[GRADS, z] = jnp.where(mine, near, turned(far)).astype(BF)
    send_own(GRADS)
    g_rows = placed(blocks[GRADS, z])

    def span_of(array, group):
        part = blocks[array, pl.ds(group * chunk, chunk)]
        return part.reshape(chunk * tokens, width)

    def logits(group):
        keys = span_of(KEYS, group)
        return [dot_nt(q_rows[f], keys) for f in range(2)]

    def highest(values):
        return jnp.max(jnp.maximum(values[0], values[1]), axis=1, keepdims=True)

    long_lane = lax.broadcasted_iota(jnp.int32, (chunk * tokens, width), 1)
    long_halves = [long_lane < HSZ, long_lane >= HSZ]

    def accumulate(group, values, first):
        held = span_of(VALUES, group).astype(F32)
        for f in range(2):
            weights = jnp.exp(values[f] - top).astype(BF)
            probs[group, f] = weights
            term = dot_nn(weights, jnp.where(long_halves[f], held, 1.0).astype(BF))
            acc[f] = term if first else acc[f] + term

    wait_all(KEYS)
    if groups == 1:
        values = logits(0)
        top = highest(values)
        wait_all(VALUES)
        accumulate(0, values, True)
    else:
        def max_step(group, carry):
            return jnp.maximum(carry, highest(logits(group)))

        top = lax.fori_loop(0, groups, max_step, jnp.full((2 * tokens, 1), -1e30, F32))
        wait_all(VALUES)
        clear(acc)

        def sum_step(group, carry):
            accumulate(group, logits(group), False)
            return carry

        lax.fori_loop(0, groups, sum_step, 0)
    both = joined()
    sums = turned(both)[:, 0:1]
    inverse = 1.0 / sums
    product = jnp.where(tall_halves[0], both * inverse, 0.0) * g_rows[0].astype(F32)
    delta = jnp.sum(product, axis=1, keepdims=True)
    norm = top + jnp.log(sums)
    columns = [norm[:tokens], norm[tokens:], delta[:tokens], delta[tokens:]]
    table = jnp.zeros((tokens, width), F32)
    for n, column in enumerate(columns):
        table = jnp.where(lane == n, column, table)
    padded = stats.shape[2]
    if padded > tokens:
        table = jnp.concatenate([table, jnp.zeros((padded - tokens, width), F32)], axis=0)
    stats[z] = table.T[: stats.shape[1]]

    def stat_copy(step):
        return pltpu.make_async_remote_copy(
            src_ref=stats.at[z],
            dst_ref=stats.at[z],
            send_sem=stat_send.at[step],
            recv_sem=stat_recv.at[z],
            device_id=(peer(step), h),
            device_id_type=MESH,
        )

    def stat_wait(slot):
        pltpu.make_async_remote_copy(
            src_ref=stats.at[slot],
            dst_ref=stats.at[slot],
            send_sem=stat_send.at[0],
            recv_sem=stat_recv.at[slot],
            device_id=(other, h),
            device_id_type=MESH,
        ).wait_recv()

    def stat_start(step, carry):
        stat_copy(step).start()
        return carry

    lax.fori_loop(1, outer, stat_start, 0)

    def return_copy(index):
        return pair_copy(
            results.at[index], returned.at[index], return_send.at[index], return_recv.at[index]
        )

    def give_back(index, value):
        results[index] = jnp.where(halves[0], value[:tokens], turned(value[tokens:])).astype(BF)
        return_copy(index).start()

    def query_block(group, first):
        keys = span_of(KEYS, group)
        held = span_of(VALUES, group)
        for f in range(2):
            slopes = dot_nt(g_rows[f], held)
            score = (probs[group, f].astype(F32) * (slopes - delta)).astype(BF)
            term = dot_nn(score, keys)
            acc[f] = term if first else acc[f] + term

    if groups == 1:
        query_block(0, True)
    else:
        clear(acc)

        def query_step(group, carry):
            query_block(group, False)
            return carry

        lax.fori_loop(0, groups, query_step, 0)
    give_back(0, joined() * (inverse * scale))

    k_rows = [(part.astype(F32) * scale).astype(BF) for part in placed(blocks[KEYS, z])]
    v_rows = placed(blocks[VALUES, z])
    for n in range(4):
        acc[n] = jnp.zeros((2 * tokens, width), F32)

    def owner_step(step, carry):
        slot = (z + step) % outer

        @pl.when(step > 0)
        def _():
            block_wait(QUERIES, slot)
            stat_wait(slot)
            block_wait(GRADS, slot)

        queries = blocks[QUERIES, slot]
        grads = blocks[GRADS, slot]
        table = stats[slot]
        for f in range(2):
            weights = jnp.exp(dot_nt(k_rows[f], queries) - table[f : f + 1, :tokens])
            slopes = dot_nt(v_rows[f], grads) - table[2 + f : 3 + f, :tokens]
            acc[f] += dot_nn((weights * slopes).astype(BF), queries)
            acc[2 + f] += dot_nn(weights.astype(BF), grads)
        return carry

    lax.fori_loop(0, outer, owner_step, 0)
    give_back(1, joined() * scale)
    give_back(2, acc[2] + turned(acc[3]))
    for index, out in enumerate((dq_ref, dk_ref, dv_ref)):
        return_copy(index).wait_recv()
        out[...] = merged(results[index], returned[index])

    for index in range(3):
        return_copy(index).wait_send()
        swap_copy(index).wait_send()
    for index, (dz, dy) in enumerate(ways):
        @pl.when(exists(dz, dy))
        def _(index=index, dz=dz, dy=dy):
            halo_copy(index, dz, dy).wait_send()
    for step in range(height):
        if step:
            piece_copy(0, step).wait_send()
        piece_copy(1, step).wait_send()

    def drain(step, carry):
        for array in range(4):
            block_copy(array, step).wait_send()
        stat_copy(step).wait_send()
        return carry

    lax.fori_loop(1, outer, drain, 0)


def hand_over(a_ref, b_ref, c_ref, a_out, b_out, c_out):
    a_out[...] = a_ref[...]
    b_out[...] = b_ref[...]
    c_out[...] = c_ref[...]


def body(mesh_sizes, queries, key_vectors, value_vectors, grad_conv, conv_weight, dec_weight):
    depth, height = mesh_sizes
    outer = depth // 2
    planes, rows, cols, channels = grad_conv.shape
    colp = round_up(cols + 1, 16)
    tokens, width = queries.shape
    assert depth % 2 == 0 and width == 2 * HSZ
    tokp = round_up((rows // 2) * (cols // 2), 16)
    features = dec_weight.shape[0]
    chunk = math.gcd(outer, 4)
    out = jax.ShapeDtypeStruct((tokens, width), BF)
    vmem = pl.BlockSpec(memory_space=pltpu.VMEM)
    hbm = pl.BlockSpec(memory_space=pl.ANY)
    dma = pltpu.SemaphoreType.DMA
    results = pl.pallas_call(
        functools.partial(kernel, depth, height),
        out_shape=(out, out, out),
        in_specs=[vmem, vmem, vmem, vmem, hbm, hbm],
        out_specs=(vmem, vmem, vmem),
        scratch_shapes=[
            pltpu.VMEM((planes + 2, rows + 2, colp, channels), BF),
            pltpu.VMEM((3 * channels, 9 * channels), BF),
            pltpu.VMEM(dec_weight.shape, BF),
            pltpu.VMEM((channels // 128, 512, 128), F32),
            pltpu.VMEM((2, features, 4 * channels), BF),
            pltpu.VMEM((planes * rows * colp, 9 * channels), BF),
            pltpu.VMEM((planes, rows, colp, channels), BF),
            pltpu.VMEM((height, tokp, width), BF),
            pltpu.VMEM((2, height, tokp, width), BF),
            pltpu.VMEM((3, tokens, width), BF),
            pltpu.VMEM((4, outer, tokens, width), BF),
            pltpu.VMEM((outer, 8, round_up(tokens, 128)), F32),
            pltpu.VMEM((outer // chunk, 2, 2 * tokens, chunk * tokens), BF),
            pltpu.VMEM((4, 2 * tokens, width), F32),
            pltpu.VMEM((3, tokens, width), BF),
            pltpu.VMEM((3, tokens, width), BF),
            dma((28,)),
            dma((8,)),
            dma((8,)),
            dma((2, height)),
            dma((2, height)),
            dma((3,)),
            dma((3,)),
            dma((4, outer)),
            dma((4, outer)),
            dma((outer,)),
            dma((outer,)),
            dma((3,)),
            dma((3,)),
        ],
        compiler_params=pltpu.CompilerParams(
            collective_id=0, has_side_effects=True, vmem_limit_bytes=58 * 2**20
        ),
        cost_estimate=pl.CostEstimate(
            flops=4 * 10**9, bytes_accessed=8 * 10**6, transcendentals=2 * 10**6
        ),
    )(queries, key_vectors, value_vectors, grad_conv, conv_weight, dec_weight)
    return pl.pallas_call(
        hand_over,
        out_shape=(out, out, out),
        in_specs=[vmem, vmem, vmem],
        out_specs=(vmem, vmem, vmem),
    )(*results)


def solution(mesh):
    in_specs = (
        P("depth", "height"),
        P("depth", "height"),
        P("depth", "height"),
        P("depth", "height", None, None),
        P(),
        P(),
    )
    out_specs = (P("depth", "height"), P("depth", "height"), P("depth", "height"))
    sizes = (mesh.shape["depth"], mesh.shape["height"])
    return jax.shard_map(
        functools.partial(body, sizes),
        mesh=mesh,
        in_specs=in_specs,
        out_specs=out_specs,
        check_vma=False,
    )
```

```python
import functools
import math

import jax
import jax.numpy as jnp
from jax import lax
from jax.experimental import pallas as pl
from jax.experimental.pallas import tpu as pltpu
from jax.sharding import PartitionSpec as P

HSZ = 64
LOSS_SCALE = 64.0
MESH = pl.DeviceIdType.MESH
BF = jnp.bfloat16
F32 = jnp.float32
KEYS, VALUES, QUERIES, GRADS = range(4)


def round_up(value, multiple):
    return (value + multiple - 1) // multiple * multiple


def dot_nt(left, right):
    return lax.dot_general(left, right, (((1,), (1,)), ((), ())), preferred_element_type=F32)


def dot_nn(left, right):
    return lax.dot_general(left, right, (((1,), (0,)), ((), ())), preferred_element_type=F32)


def selection(shape, runs):
    row = lax.broadcasted_iota(jnp.int32, shape, 0)
    col = lax.broadcasted_iota(jnp.int32, shape, 1)
    chosen = None
    for first, count, start, step in runs:
        hit = (row >= first) & (row < first + count) & (col == start + step * (row - first))
        chosen = hit if chosen is None else chosen | hit
    return chosen.astype(F32).astype(BF)


def kernel(
    depth, height,
    q_ref, k_ref, v_ref, x_ref, w_hbm, d_hbm,
    dq_ref, dk_ref, dv_ref,
    halo, w_ref, d_raw, d_tall, d_ref, windows, voxels, pieces, landed, swapped, blocks, stats, probs,
    acc, results, returned,
    load_sems, halo_send, halo_recv, piece_send, piece_recv, swap_send, swap_recv,
    own_send, block_recv, stat_send, stat_recv, return_send, return_recv,
):
    planes, rows, cols, channels = x_ref.shape
    colp = halo.shape[2]
    tokens, width = q_ref.shape
    scale = 1.0 / math.sqrt(HSZ)
    outer = depth // 2
    groups, chunk = probs.shape[0], outer // probs.shape[0]
    tok_rows, tok_cols = rows // 2, cols // 2
    toks = tok_rows * tok_cols
    tokp = pieces.shape[1]

    d = lax.axis_index("depth")
    h = lax.axis_index("height")
    z, x = d // 2, d % 2
    other = 2 * z + (1 - x)

    taps = [(i, j) for i in range(3) for j in range(3)]
    load_d = pltpu.make_async_copy(d_hbm, d_raw, load_sems.at[27])
    load_d.start()
    loads_w = []
    for n, (i, j) in enumerate(taps):
        for l in range(3):
            loads_w.append(
                pltpu.make_async_copy(
                    w_hbm.at[i, j, l],
                    w_ref.at[pl.ds(l * channels, channels), pl.ds(n * channels, channels)],
                    load_sems.at[3 * n + l],
                )
            )
    for load in loads_w:
        load.start()

    halo[...] = jnp.zeros_like(halo)
    halo[1 : 1 + planes, 1 : 1 + rows, 0:cols, :] = x_ref[...]

    barrier = pltpu.get_barrier_semaphore()

    def greet(dd, hh):
        pl.semaphore_signal(barrier, inc=1, device_id=(dd, hh), device_id_type=MESH)

    def peer(step):
        return ((z + step) % outer) * 2 + x

    greet(other, h)
    for step in range(1, height):
        greet(d, (h + step) % height)
        greet(other, (h + step) % height)

    def greet_line(step, carry):
        greet(peer(step), h)
        return carry

    lax.fori_loop(1, outer, greet_line, 0)
    corners = [(dz, dy) for dz in (-1, 1) for dy in (-1, 1)]
    ways = [(dz, 0) for dz in (-1, 1)] + [(0, dy) for dy in (-1, 1)] + corners

    def exists(dz, dy):
        found = None
        for delta, place, extent in ((dz, d, depth), (dy, h, height)):
            if delta:
                here = (place + delta >= 0) & (place + delta < extent)
                found = here if found is None else found & here
        return found

    count = 1 + 2 * (height - 1) + (outer - 1)
    for dz, dy in ways:
        if dz == 0:
            continue
        there = exists(dz, dy)
        count = count + jnp.where(there, 1, 0)

        @pl.when(there)
        def _(dz=dz, dy=dy):
            greet(d + dz, h + dy)

    pl.semaphore_wait(barrier, count)

    def span(delta, extent, receiving):
        if delta == 0:
            return pl.ds(1, extent)
        if receiving:
            return pl.ds(0 if delta > 0 else extent + 1, 1)
        return pl.ds(extent if delta > 0 else 1, 1)

    def halo_copy(index, dz, dy):
        return pltpu.make_async_remote_copy(
            src_ref=halo.at[span(dz, planes, False), span(dy, rows, False)],
            dst_ref=halo.at[span(dz, planes, True), span(dy, rows, True)],
            send_sem=halo_send.at[index],
            recv_sem=halo_recv.at[index],
            device_id=(d + dz, h + dy),
            device_id_type=MESH,
        )

    def pair_copy(source, target, send_sem, recv_sem):
        return pltpu.make_async_remote_copy(
            src_ref=source,
            dst_ref=target,
            send_sem=send_sem,
            recv_sem=recv_sem,
            device_id=(other, h),
            device_id_type=MESH,
        )

    def swap_copy(array):
        return pair_copy(
            sources[array], swapped.at[array], swap_send.at[array], swap_recv.at[array]
        )

    sources = {KEYS: k_ref, VALUES: v_ref, QUERIES: q_ref}
    for array in (KEYS, VALUES, QUERIES):
        swap_copy(array).start()
    for index, (dz, dy) in enumerate(ways):
        @pl.when(exists(dz, dy))
        def _(index=index, dz=dz, dy=dy):
            halo_copy(index, dz, dy).start()

    lane = lax.broadcasted_iota(jnp.int32, (tokens, width), 1)
    tall_lane = lax.broadcasted_iota(jnp.int32, (2 * tokens, width), 1)
    halves = [lane < HSZ, lane >= HSZ]
    tall_halves = [tall_lane < HSZ, tall_lane >= HSZ]
    mine = (lane >= x * HSZ) & (lane < (x + 1) * HSZ)

    def turned(value):
        return pltpu.roll(value, HSZ, 1)

    def merged(own, received):
        return jnp.where(mine, own.astype(F32), turned(received.astype(F32))).astype(BF)

    def block_copy(array, step):
        return pltpu.make_async_remote_copy(
            src_ref=blocks.at[array, z],
            dst_ref=blocks.at[array, z],
            send_sem=own_send.at[array, step],
            recv_sem=block_recv.at[array, z],
            device_id=(peer(step), h),
            device_id_type=MESH,
        )

    def block_wait(array, slot):
        pltpu.make_async_remote_copy(
            src_ref=blocks.at[array, slot],
            dst_ref=blocks.at[array, slot],
            send_sem=own_send.at[array, 0],
            recv_sem=block_recv.at[array, slot],
            device_id=(other, h),
            device_id_type=MESH,
        ).wait_recv()

    def send_own(array):
        def one(step, carry):
            block_copy(array, step).start()
            return carry
        lax.fori_loop(1, outer, one, 0)

    def wait_all(array):
        def one(step, carry):
            block_wait(array, (z + step) % outer)
            return carry
        lax.fori_loop(1, outer, one, 0)

    for array in (KEYS, VALUES, QUERIES):
        swap_copy(array).wait_recv()
        blocks[array, z] = merged(sources[array][...], swapped[array])
        send_own(array)

    load_d.wait()
    features = d_raw.shape[0]
    part_len = d_tall.shape[1] // 8
    for start in range(0, features, part_len):
        wide = d_raw[start : start + part_len].astype(F32).reshape(part_len * 8, channels)
        for lanes in range(d_tall.shape[0]):
            d_tall[lanes] = wide[:, lanes * 128 : (lanes + 1) * 128]
        for s in range(8):
            for lanes in range(d_tall.shape[0]):
                place = (s // 2) * channels + lanes * 128
                d_ref[s % 2, start : start + part_len, place : place + 128] = d_tall[
                    lanes, pl.ds(s, part_len, stride=8), :
                ].astype(BF)

    for index, (dz, dy) in enumerate(ways):
        @pl.when(exists(-dz, -dy))
        def _(index=index, dz=dz, dy=dy):
            halo_copy(index, dz, dy).wait_recv()
    for load in loads_w:
        load.wait()
    flat = planes * rows * colp
    for n, (i, j) in enumerate(taps):
        window = halo[2 - i : 2 - i + planes, 2 - j : 2 - j + rows]
        windows[:, n * channels : (n + 1) * channels] = window.reshape(flat, channels)
    sums = dot_nt(windows[...], w_ref[...])
    total = (
        pltpu.roll(sums[:, :channels], flat - 1, 0)
        + sums[:, channels : 2 * channels]
        + pltpu.roll(sums[:, 2 * channels :], 1, 0)
    )
    voxels[...] = (LOSS_SCALE * total).astype(BF).reshape(planes, rows, colp, channels)

    lhs = jnp.concatenate(
        [
            jnp.concatenate([voxels[a, 2 * t + b] for t in range(tok_rows)], axis=0)
            for a in range(2)
            for b in range(2)
        ],
        axis=1,
    )
    parts = [dot_nt(lhs, d_ref[c]) for c in range(2)]
    total = parts[0] + pltpu.roll(parts[1], tok_rows * colp - 1, 0)
    pick = selection(
        (tokp, tok_rows * colp), [(t * tok_cols, tok_cols, t * colp, 2) for t in range(tok_rows)]
    )
    compact = dot_nn(pick, total.astype(BF)).astype(BF)
    for hh in range(height):
        pieces[hh] = compact[:, hh * width : (hh + 1) * width]

    def piece_copy(away, step):
        target = (h + step) % height
        return pltpu.make_async_remote_copy(
            src_ref=pieces.at[target],
            dst_ref=landed.at[away, h],
            send_sem=piece_send.at[away, step],
            recv_sem=piece_recv.at[away, h],
            device_id=(other if away else d, target),
            device_id_type=MESH,
        )

    def piece_wait(away, slot):
        pltpu.make_async_remote_copy(
            src_ref=landed.at[away, slot],
            dst_ref=landed.at[away, slot],
            send_sem=piece_send.at[away, 0],
            recv_sem=piece_recv.at[away, slot],
            device_id=(other, h),
            device_id_type=MESH,
        ).wait_recv()

    for step in range(height):
        if step:
            piece_copy(0, step).start()
        piece_copy(1, step).start()
    landed[0, h] = pieces[h]

    def placed(block):
        wide = block.astype(F32)
        low = [jnp.where(half, wide, 0.0) for half in halves]
        return [
            jnp.concatenate([low[0], turned(low[1])], axis=0).astype(BF),
            jnp.concatenate([turned(low[0]), low[1]], axis=0).astype(BF),
        ]

    def joined():
        return acc[0] + turned(acc[1])

    def clear(which):
        for f in range(2):
            which[f] = jnp.zeros((2 * tokens, width), F32)

    q_rows = [(part.astype(F32) * scale).astype(BF) for part in placed(blocks[QUERIES, z])]

    for step in range(1, height):
        piece_wait(0, (h + step) % height)
    for step in range(height):
        piece_wait(1, (h + step) % height)
    spread = selection((tokens, height * tokp), [(s * toks, toks, s * tokp, 1) for s in range(height)])
    near, far = [
        dot_nn(spread, landed[away].reshape(height * tokp, width)) for away in range(2)
    ]
    blocks[GRADS, z] = jnp.where(mine, near, turned(far)).astype(BF)
    send_own(GRADS)
    g_rows = placed(blocks[GRADS, z])

    def span_of(array, group):
        part = blocks[array, pl.ds(group * chunk, chunk)]
        return part.reshape(chunk * tokens, width)

    def logits(group):
        keys = span_of(KEYS, group)
        return [dot_nt(q_rows[f], keys) for f in range(2)]

    def highest(values):
        return jnp.max(jnp.maximum(values[0], values[1]), axis=1, keepdims=True)

    long_lane = lax.broadcasted_iota(jnp.int32, (chunk * tokens, width), 1)
    long_halves = [long_lane < HSZ, long_lane >= HSZ]

    def accumulate(group, values, first):
        held = span_of(VALUES, group).astype(F32)
        for f in range(2):
            weights = jnp.exp(values[f] - top).astype(BF)
            probs[group, f] = weights
            term = dot_nn(weights, jnp.where(long_halves[f], held, 1.0).astype(BF))
            acc[f] = term if first else acc[f] + term

    wait_all(KEYS)
    if groups == 1:
        values = logits(0)
        top = highest(values)
        wait_all(VALUES)
        accumulate(0, values, True)
    else:
        def max_step(group, carry):
            return jnp.maximum(carry, highest(logits(group)))

        top = lax.fori_loop(0, groups, max_step, jnp.full((2 * tokens, 1), -1e30, F32))
        wait_all(VALUES)
        clear(acc)

        def sum_step(group, carry):
            accumulate(group, logits(group), False)
            return carry

        lax.fori_loop(0, groups, sum_step, 0)
    both = joined()
    sums = turned(both)[:, 0:1]
    inverse = 1.0 / sums
    product = jnp.where(tall_halves[0], both * inverse, 0.0) * g_rows[0].astype(F32)
    delta = jnp.sum(product, axis=1, keepdims=True)
    norm = top + jnp.log(sums)
    columns = [norm[:tokens], norm[tokens:], delta[:tokens], delta[tokens:]]
    table = jnp.zeros((tokens, width), F32)
    for n, column in enumerate(columns):
        table = jnp.where(lane == n, column, table)
    padded = stats.shape[2]
    if padded > tokens:
        table = jnp.concatenate([table, jnp.zeros((padded - tokens, width), F32)], axis=0)
    stats[z] = table.T[: stats.shape[1]]

    def stat_copy(step):
        return pltpu.make_async_remote_copy(
            src_ref=stats.at[z],
            dst_ref=stats.at[z],
            send_sem=stat_send.at[step],
            recv_sem=stat_recv.at[z],
            device_id=(peer(step), h),
            device_id_type=MESH,
        )

    def stat_wait(slot):
        pltpu.make_async_remote_copy(
            src_ref=stats.at[slot],
            dst_ref=stats.at[slot],
            send_sem=stat_send.at[0],
            recv_sem=stat_recv.at[slot],
            device_id=(other, h),
            device_id_type=MESH,
        ).wait_recv()

    def stat_start(step, carry):
        stat_copy(step).start()
        return carry

    lax.fori_loop(1, outer, stat_start, 0)

    def return_copy(index):
        return pair_copy(
            results.at[index], returned.at[index], return_send.at[index], return_recv.at[index]
        )

    def give_back(index, value):
        results[index] = jnp.where(halves[0], value[:tokens], turned(value[tokens:])).astype(BF)
        return_copy(index).start()

    def query_block(group, first):
        keys = span_of(KEYS, group)
        held = span_of(VALUES, group)
        for f in range(2):
            slopes = dot_nt(g_rows[f], held)
            score = (probs[group, f].astype(F32) * (slopes - delta)).astype(BF)
            term = dot_nn(score, keys)
            acc[f] = term if first else acc[f] + term

    if groups == 1:
        query_block(0, True)
    else:
        clear(acc)

        def query_step(group, carry):
            query_block(group, False)
            return carry

        lax.fori_loop(0, groups, query_step, 0)
    give_back(0, joined() * (inverse * scale))

    k_rows = [(part.astype(F32) * scale).astype(BF) for part in placed(blocks[KEYS, z])]
    v_rows = placed(blocks[VALUES, z])
    for n in range(4):
        acc[n] = jnp.zeros((2 * tokens, width), F32)

    def owner_step(step, carry):
        slot = (z + step) % outer

        @pl.when(step > 0)
        def _():
            block_wait(QUERIES, slot)
            stat_wait(slot)
            block_wait(GRADS, slot)

        queries = blocks[QUERIES, slot]
        grads = blocks[GRADS, slot]
        table = stats[slot]
        for f in range(2):
            weights = jnp.exp(dot_nt(k_rows[f], queries) - table[f : f + 1, :tokens])
            slopes = dot_nt(v_rows[f], grads) - table[2 + f : 3 + f, :tokens]
            acc[f] += dot_nn((weights * slopes).astype(BF), queries)
            acc[2 + f] += dot_nn(weights.astype(BF), grads)
        return carry

    lax.fori_loop(0, outer, owner_step, 0)
    give_back(1, joined() * scale)
    give_back(2, acc[2] + turned(acc[3]))
    for index, out in enumerate((dq_ref, dk_ref, dv_ref)):
        return_copy(index).wait_recv()
        out[...] = merged(results[index], returned[index])

    for index in range(3):
        return_copy(index).wait_send()
        swap_copy(index).wait_send()
    for index, (dz, dy) in enumerate(ways):
        @pl.when(exists(dz, dy))
        def _(index=index, dz=dz, dy=dy):
            halo_copy(index, dz, dy).wait_send()
    for step in range(height):
        if step:
            piece_copy(0, step).wait_send()
        piece_copy(1, step).wait_send()

    def drain(step, carry):
        for array in range(4):
            block_copy(array, step).wait_send()
        stat_copy(step).wait_send()
        return carry

    lax.fori_loop(1, outer, drain, 0)


def hand_over(a_ref, b_ref, c_ref, a_out, b_out, c_out):
    a_out[...] = a_ref[...]
    b_out[...] = b_ref[...]
    c_out[...] = c_ref[...]


def body(mesh_sizes, queries, key_vectors, value_vectors, grad_conv, conv_weight, dec_weight):
    depth, height = mesh_sizes
    outer = depth // 2
    planes, rows, cols, channels = grad_conv.shape
    colp = round_up(cols + 1, 16)
    tokens, width = queries.shape
    assert depth % 2 == 0 and width == 2 * HSZ
    tokp = round_up((rows // 2) * (cols // 2), 16)
    features = dec_weight.shape[0]
    chunk = math.gcd(outer, 4)
    out = jax.ShapeDtypeStruct((tokens, width), BF)
    vmem = pl.BlockSpec(memory_space=pltpu.VMEM)
    hbm = pl.BlockSpec(memory_space=pl.ANY)
    dma = pltpu.SemaphoreType.DMA
    results = pl.pallas_call(
        functools.partial(kernel, depth, height),
        out_shape=(out, out, out),
        in_specs=[vmem, vmem, vmem, vmem, hbm, hbm],
        out_specs=(vmem, vmem, vmem),
        scratch_shapes=[
            pltpu.VMEM((planes + 2, rows + 2, colp, channels), BF),
            pltpu.VMEM((3 * channels, 9 * channels), BF),
            pltpu.VMEM(dec_weight.shape, BF),
            pltpu.VMEM((channels // 128, 512, 128), F32),
            pltpu.VMEM((2, features, 4 * channels), BF),
            pltpu.VMEM((planes * rows * colp, 9 * channels), BF),
            pltpu.VMEM((planes, rows, colp, channels), BF),
            pltpu.VMEM((height, tokp, width), BF),
            pltpu.VMEM((2, height, tokp, width), BF),
            pltpu.VMEM((3, tokens, width), BF),
            pltpu.VMEM((4, outer, tokens, width), BF),
            pltpu.VMEM((outer, 8, round_up(tokens, 128)), F32),
            pltpu.VMEM((outer // chunk, 2, 2 * tokens, chunk * tokens), BF),
            pltpu.VMEM((4, 2 * tokens, width), F32),
            pltpu.VMEM((3, tokens, width), BF),
            pltpu.VMEM((3, tokens, width), BF),
            dma((28,)),
            dma((8,)),
            dma((8,)),
            dma((2, height)),
            dma((2, height)),
            dma((3,)),
            dma((3,)),
            dma((4, outer)),
            dma((4, outer)),
            dma((outer,)),
            dma((outer,)),
            dma((3,)),
            dma((3,)),
        ],
        compiler_params=pltpu.CompilerParams(
            collective_id=0, has_side_effects=True, vmem_limit_bytes=58 * 2**20
        ),
        cost_estimate=pl.CostEstimate(
            flops=4 * 10**9, bytes_accessed=8 * 10**6, transcendentals=2 * 10**6
        ),
    )(queries, key_vectors, value_vectors, grad_conv, conv_weight, dec_weight)
    return pl.pallas_call(
        hand_over,
        out_shape=(out, out, out),
        in_specs=[vmem, vmem, vmem],
        out_specs=(vmem, vmem, vmem),
    )(*results)


def solution(mesh):
    in_specs = (
        P("depth", "height"),
        P("depth", "height"),
        P("depth", "height"),
        P("depth", "height", None, None),
        P(),
        P(),
    )
    out_specs = (P("depth", "height"), P("depth", "height"), P("depth", "height"))
    sizes = (mesh.shape["depth"], mesh.shape["height"])
    return jax.shard_map(
        functools.partial(body, sizes),
        mesh=mesh,
        in_specs=in_specs,
        out_specs=out_specs,
        check_vma=False,
    )
```
